128 devices in a mesh: ctx: 32 (over x, z, y_lo), uly: 4 (over y_hi, core).
Axes of the slice: x: 4, y: 4 (y_hi: 2, y_lo: 2; y = y_hi * 2 + y_lo), z: 4, core: 2. Of those that a mesh axis runs over, the one named last changes fastest.
Arguments:
- queries: bfloat16 [16384, 24, 128], P(('ctx', 'uly')), may hold values from -6 to 6
- keys: bfloat16 [16384, 4, 128], P(('ctx', 'uly')), may hold values from -6 to 6
- values: bfloat16 [16384, 4, 128], P(('ctx', 'uly')), may hold values from -6 to 6
- stretch_tokens: int32 [4], replicated, may hold values from 2048 to 6144, as said below
- block_order: int32 [64], replicated, may hold values from 0 to 63, as said below
Outputs:
- attended: bfloat16 [16384, 3072], P(('ctx', 'uly'))
The draws below stay inside these ranges and needn't reach their ends.
Inputs may be any that keep to these rules, and one draw needn't show every extreme that they name: `block_order`: every block appears once; slots 2 * c and 2 * c + 1 hold blocks b and 63 - b. `stretch_tokens`: the lengths sum to 16384; at least one stretch has 6144 tokens.
All inputs are finite; a program needn't handle non-finite values.
Results may differ from the reference program's by a relative error of at most 0.006.
Values may be sent and summed in bfloat16 or wider, within the bound.
A program may use at most 128 MiB of HBM per device.

```python
import math
import jax
import jax.numpy as jnp
from jax import lax

HEAD_SIZE = 128
HQ = 24
KEY_VALUE_HEADS = 4
QUERY_PER_KEY = 6
TOKEN_COUNT = 16384
BLOCKS = 64
BLOCK = 256


def draw_queries(key, part):
    key = jax.random.fold_in(key, 5)
    unmasked_part = jnp.clip(1.6 * jax.random.normal(key, (TOKEN_COUNT, HQ, HEAD_SIZE), jnp.float32), -6.0, 6.0)
    return unmasked_part.astype(jnp.bfloat16)


def draw_keys(key, part):
    key = jax.random.fold_in(key, 7)
    unmasked_part = jnp.clip(1.6 * jax.random.normal(key, (TOKEN_COUNT, KEY_VALUE_HEADS, HEAD_SIZE), jnp.float32), -6.0, 6.0)
    return unmasked_part.astype(jnp.bfloat16)


def draw_stretch_tokens(key, part):
    key = jax.random.fold_in(key, 11)
    cut_key, order_key = jax.random.split(key)
    spare = TOKEN_COUNT // 4
    cuts = jax.random.randint(cut_key, (2,), 0, spare + 1).astype(jnp.int32)
    lower = jnp.minimum(cuts[0], cuts[1])
    upper = jnp.maximum(cuts[0], cuts[1])
    extras = jnp.stack([spare, lower, upper - lower, spare - upper]).astype(jnp.int32)
    lengths = (TOKEN_COUNT // 8 + extras).astype(jnp.int32)
    return jax.random.permutation(order_key, lengths).astype(jnp.int32)


def draw_block_order(key, part):
    key = jax.random.fold_in(key, 9)
    halves = jax.random.permutation(key, BLOCKS // 2).astype(jnp.int32)
    paired = jnp.stack([halves, BLOCKS - 1 - halves], axis=1)
    return paired.reshape(BLOCKS).astype(jnp.int32)


def block_levels(stream_key, extent, cuts, low, high):
    level = 1.0
    for axis_at, blocks in cuts:
        heights = jax.random.uniform(jax.random.fold_in(jax.random.fold_in(stream_key, 6), axis_at), (blocks,), jnp.float32, low / len(cuts), high / len(cuts))
        level = level * jnp.repeat(jnp.exp(heights), extent[axis_at] // blocks).reshape((-1,) + (1,) * (len(extent) - 1 - axis_at))
    return level


def noise(key, shape, width, bound, cuts=(), held_as=jnp.bfloat16):
    result = jax.random.normal(key, shape, jnp.float32) * width
    if len(cuts) > 0:
        result = block_levels(key, shape, cuts, -0.22, 0.18) * result
    return jnp.clip(result, min=-bound, max=bound).astype(held_as)


def setup_inputs(seed: int = 0) -> dict:
    key_of = jax.random.split(jax.random.key(seed), 6)
    queries = draw_queries(jax.random.fold_in(key_of[5], 71), 0)
    keys = draw_keys(jax.random.fold_in(key_of[5], 71), 0)
    values = noise(key_of[2], (TOKEN_COUNT, KEY_VALUE_HEADS, HEAD_SIZE), 1.0, 6.0, ((0, 128),))
    stretch_tokens = draw_stretch_tokens(jax.random.fold_in(key_of[5], 71), 0)
    block_order = draw_block_order(jax.random.fold_in(key_of[5], 71), 0)
    return dict(queries=queries, keys=keys, values=values, stretch_tokens=stretch_tokens, block_order=block_order)


def stretch_lookup(positions, stretch_tokens):
    stretch_ends = jnp.cumsum(stretch_tokens).astype(jnp.int32)
    return jnp.sum((stretch_ends[None, :] <= positions[:, None]).astype(jnp.int32), axis=1).astype(jnp.int32)


def reference(queries, keys, values, stretch_tokens, block_order):
    row_ids = jnp.arange(TOKEN_COUNT, dtype=jnp.int32)
    slot_index = (row_ids // BLOCK).astype(jnp.int32)
    positions = (block_order[slot_index] * BLOCK + row_ids % BLOCK).astype(jnp.int32)
    stretch = stretch_lookup(positions, stretch_tokens)
    row_block_index = math.gcd(TOKEN_COUNT, 512)
    count_of_blocks = TOKEN_COUNT // row_block_index
    grouped_queries = queries.reshape(TOKEN_COUNT, KEY_VALUE_HEADS, QUERY_PER_KEY, HEAD_SIZE)
    score_scale = HEAD_SIZE ** -0.5

    def tokens_per_block(flattened_index):
        index_of_block = flattened_index // KEY_VALUE_HEADS
        key_value_head = flattened_index % KEY_VALUE_HEADS
        first_row = (index_of_block * row_block_index).astype(jnp.int32)
        query_part = lax.dynamic_slice_in_dim(grouped_queries, first_row, row_block_index, 0)
        query_part = lax.dynamic_index_in_dim(query_part, key_value_head, 1, keepdims=False)
        key_part = lax.dynamic_index_in_dim(keys, key_value_head, 1, keepdims=False)
        value_part = lax.dynamic_index_in_dim(values, key_value_head, 1, keepdims=False)
        query_stretch = lax.dynamic_slice_in_dim(stretch, first_row, row_block_index, 0)
        scores = jnp.einsum("qgd,kd->gqk", query_part.astype(jnp.float32), key_part.astype(jnp.float32)) * score_scale
        visible = stretch[None, :] <= query_stretch[:, None]
        masked = jnp.where(visible[None], scores, -1e30)
        rowmax = jnp.max(masked, axis=-1, keepdims=True)
        weights = jnp.where(visible[None], jnp.exp(masked - rowmax), 0.0)
        denominator = jnp.sum(weights, axis=-1)
        rounded = lax.optimization_barrier(weights.astype(jnp.bfloat16)).astype(jnp.float32)
        numerator = jnp.einsum("gqk,kd->qgd", rounded, value_part.astype(jnp.float32))
        return numerator / jnp.transpose(denominator)[:, :, None]

    output_list = lax.map(tokens_per_block, jnp.arange(count_of_blocks * KEY_VALUE_HEADS, dtype=jnp.int32))
    output_list = output_list.reshape(count_of_blocks, KEY_VALUE_HEADS, row_block_index, QUERY_PER_KEY, HEAD_SIZE)
    output_list = jnp.transpose(output_list, (0, 2, 1, 3, 4)).reshape(TOKEN_COUNT, HQ * HEAD_SIZE)
    return output_list.astype(jnp.bfloat16)
```

```python
import functools

import jax
import jax.numpy as jnp
from jax import lax
from jax.experimental import pallas as pl
from jax.experimental.pallas import tpu as pltpu
from jax.sharding import PartitionSpec as P

MESH = pl.DeviceIdType.MESH
F32 = jnp.float32
BF16 = jnp.bfloat16

D = 128
G = 6
HALF = 128
SLOTS = 64
SLOT = 256
COLUMN = 1024
LATE = 2 * G * HALF
TOKENS = SLOTS * SLOT
TO_LOG2 = (D**-0.5) * 1.4426950408889634
HIDDEN = -30000.0
SHIFT_LANE = 4
TOO_LARGE = 1e30
VMEM_LIMIT = 60 * 2**20


def div(a, n):
    return lax.div(a, n)


def rem(a, n):
    return lax.rem(a, n)


def place():
    ctx, uly = lax.axis_index("ctx"), lax.axis_index("uly")
    return div(ctx, 8), div(uly, 2) * 2 + rem(ctx, 2), rem(div(ctx, 2), 4), rem(uly, 2)


def device_at(x, y, z, core):
    return (x * 8 + z * 2 + rem(y, 2), div(y, 2) * 2 + core)


def slot_in_column(chip):
    return 2 * rem(chip, 2) + div(chip, 2)


def stretch_ends(tokens_ref):
    first = tokens_ref[0]
    second = first + tokens_ref[1]
    return first, second, second + tokens_ref[2]


def stretch_of(position, ends):
    total = (position >= ends[0]).astype(jnp.int32)
    for end in ends[1:]:
        total = total + (position >= end).astype(jnp.int32)
    return total


def key_columns(first_position, rows, ends):
    position = first_position + lax.broadcasted_iota(jnp.int32, (rows, D), 0)
    lane = lax.broadcasted_iota(jnp.int32, (rows, D), 1)
    hidden = jnp.where(lane < stretch_of(position, ends), HIDDEN, 0.0)
    return jnp.where(lane == SHIFT_LANE, 1.0, hidden).astype(BF16)


def query_columns(first_position, rows, ends):
    position = first_position + lax.broadcasted_iota(jnp.int32, (rows, D), 0)
    lane = lax.broadcasted_iota(jnp.int32, (rows, D), 1)
    return jnp.where(lane == stretch_of(position, ends), 1.0, 0.0)


def lane_sum(x):
    total = x[:, :D]
    for j in range(1, x.shape[1] // D):
        total = total + x[:, j * D : (j + 1) * D]
    return total


def lane_max(x):
    total = x[:, :D]
    for j in range(1, x.shape[1] // D):
        total = jnp.maximum(total, x[:, j * D : (j + 1) * D])
    return total


def scores_of(q, k):
    return lax.dot_general(q, k, (((1,), (1,)), ((), ())), preferred_element_type=F32)


def attend(rows, query_ref, k, v, sum_ref, total_ref):
    weights = jnp.exp2(scores_of(query_ref[rows, :], k) * TO_LOG2)
    sum_ref[rows, :] += lane_sum(weights)
    total_ref[rows, :] += jnp.dot(weights.astype(BF16), v, preferred_element_type=F32)


def set_shift(query_ref, k, rows_per_step):
    for first in range(0, query_ref.shape[0], rows_per_step):
        rows = slice(first, first + rows_per_step)
        largest = jnp.max(lane_max(scores_of(query_ref[rows, :], k)), axis=1, keepdims=True)
        lane = lax.broadcasted_iota(jnp.int32, (rows_per_step, D), 1)
        old = query_ref[rows, D:].astype(F32)
        query_ref[rows, D:] = jnp.where(lane == SHIFT_LANE, -largest, old).astype(BF16)


def gather_kernel(
    tokens_ref,
    order_ref,
    q_ref,
    kv_ref,
    late_ref,
    largest_ref,
    q_out,
    kv_out,
    kv,
    columns,
    q_all,
    query,
    total,
    sums,
    local_sem,
    out_sem,
    line_send,
    line_recv,
    ring_send,
    ring_recv,
    pair_send,
    pair_recv,
):
    x, y, z, core = place()
    other = 1 - core
    column = 4 * x + z
    ends = stretch_ends(tokens_ref)

    def column_at(dx, dz):
        return rem(x + dx, 4) * 4 + rem(z + dz, 4)

    def along(da, db):
        return da * (1 - core) + db * core, da * core + db * (1 - core)

    def chunk(da, db):
        return column_at(*along(da, db)) * 4

    def device_along(da, db):
        dx, dz = along(da, db)
        return device_at(rem(x + dx, 4), y, rem(z + dz, 4), core)

    line = [device_at(x, rem(y + d, 4), z, core) for d in (1, 2, 3)]
    ring = [device_along(*o) for o in ((1, 0), (3, 0), (0, 1), (0, 3))]
    sibling = device_at(x, y, z, other)

    barrier = pltpu.get_barrier_semaphore()
    for partner in (*line, *ring, sibling):
        pl.semaphore_signal(barrier, inc=1, device_id=partner, device_id_type=MESH)
    pl.semaphore_wait(barrier, 8)

    sent = []

    def send(make):
        pltpu.make_async_remote_copy(*make(), device_id_type=MESH).start()
        sent.append(make)

    own_slot = column * 4 + slot_in_column(y)
    for d in (1, 3, 2):
        send(
            lambda d=d: (
                kv_ref.at[rem(y + d, 4)],
                kv.at[:, own_slot, core],
                line_send.at[0, d - 1],
                line_recv.at[0, d - 1],
                line[d - 1],
            )
        )
    own_kv = pltpu.make_async_copy(kv_ref.at[y], kv.at[:, own_slot, core], local_sem.at[0])
    own_kv.start()
    for d in (1, 3, 2):
        send(
            lambda d=d: (
                q_ref.at[pl.ds(G * rem(y + d, 4), G)],
                q_all.at[y],
                line_send.at[1, d - 1],
                line_recv.at[1, d - 1],
                line[d - 1],
            )
        )
    own_q = pltpu.make_async_copy(q_ref.at[pl.ds(G * y, G)], q_all.at[y], local_sem.at[1])
    own_q.start()

    def arrived(dst, sem):
        pltpu.make_async_copy(dst, dst, sem).wait()

    def part(which, da, db):
        if which is None:
            return kv.at[:, pl.ds(chunk(da, db), 4), core]
        return kv.at[which, pl.ds(chunk(da, db), 4), core]

    def hop(which, da, db, step_a, step_b, there_a, there_b):
        direction = (1 if step_a + step_b > 0 else 0) + (2 if step_b != 0 else 0)

        def make():
            src = part(which, da, db)
            return (
                src,
                src,
                ring_send.at[da * 4 + db, direction],
                ring_recv.at[there_a * 4 + there_b, 0 if which is None else which],
                device_along(step_a % 4, step_b % 4),
            )

        send(make)

    def spread_a():
        hop(None, 0, 0, 1, 0, 3, 0)
        hop(None, 0, 0, -1, 0, 1, 0)

    def spread_b(da):
        hop(None, da, 0, 0, 1, da, 3)
        hop(None, da, 0, 0, -1, da, 1)

    def take(da, db):
        at = da * 4 + db
        if db == 2 or (db == 0 and da == 2):
            arrived(part(0, da, db), ring_recv.at[at, 0])
            arrived(part(1, da, db), ring_recv.at[at, 1])
        else:
            arrived(part(None, da, db), ring_recv.at[at, 0])
        if db == 3:
            hop(0, da, 3, 0, 1, da, 2)
        elif db == 1:
            hop(1, da, 1, 0, -1, da, 2)
        elif db == 0 and da == 3:
            hop(0, 3, 0, 1, 0, 2, 0)
        elif db == 0 and da == 1:
            hop(1, 1, 0, -1, 0, 2, 0)

    def share(da, db):
        def make():
            dx, dz = along(da, db)
            src = part(None, da, db)
            at = dx * 4 + dz
            return src, src, pair_send.at[at], pair_recv.at[at], sibling

        send(make)

    def stage_0():
        spread_a()
        spread_b(0)
        share(0, 0)

    def stage_1():
        take(3, 0)
        spread_b(3)
        take(1, 0)
        spread_b(1)
        take(0, 3)
        take(0, 1)
        for offset in ((3, 0), (1, 0), (0, 3), (0, 1)):
            share(*offset)

    def stage_2():
        take(2, 0)
        spread_b(2)
        take(0, 2)
        share(2, 0)
        share(0, 2)
        for offset in ((3, 3), (3, 1), (1, 3), (1, 1)):
            take(*offset)
            share(*offset)

    def stage_3():
        for offset in ((2, 3), (2, 1), (3, 2), (1, 2)):
            take(*offset)
            share(*offset)

    def stage_4():
        take(2, 2)
        share(2, 2)

    for d in (1, 3, 2):
        from_slot = column * 4 + slot_in_column(rem(y + 4 - d, 4))
        arrived(kv.at[:, from_slot, core], line_recv.at[0, d - 1])
    own_kv.wait()
    stage_0()

    @pl.loop(0, SLOTS)
    def _(slot):
        rows = pl.ds(pl.multiple_of(slot * SLOT, SLOT), SLOT)
        columns[rows, :] = key_columns(order_ref[slot] * SLOT, SLOT, ends)

    total[...] = jnp.zeros_like(total)
    sums[...] = jnp.zeros_like(sums)

    for d in (1, 3, 2):
        arrived(q_all.at[rem(y + 4 - d, 4)], line_recv.at[1, d - 1])
    own_q.wait()
    q_copy = pltpu.make_async_copy(q_all, q_out, local_sem.at[2])
    q_copy.start()
    for pair in range(2):
        first = order_ref[column * 4 + 2 * pair]
        second = order_ref[column * 4 + 2 * pair + 1]
        take_second = (second > first).astype(F32)
        extra = query_columns(jnp.maximum(first, second) * SLOT + core * HALF, HALF, ends)
        for g in range(G):
            rows = slice((pair * G + g) * HALF, (pair * G + g + 1) * HALF)
            query[rows, :D] = (
                q_all[pair, g].astype(F32) * (1.0 - take_second)
                + q_all[pair + 2, g].astype(F32) * take_second
            ).astype(BF16)
            query[rows, D:] = extra.astype(BF16)

    stage_1()

    def keys_at(at):
        k = kv[0, pl.ds(at * 4, 4)].reshape(COLUMN, D)
        extra = columns[pl.ds(pl.multiple_of(at * COLUMN, COLUMN), COLUMN), :]
        return jnp.concatenate([k, extra], axis=1)

    arrived(part_of_sibling(kv, column, other), pair_recv.at[0])
    set_shift(query, keys_at(column), LATE // 2)

    def gray(u):
        return u + div(u, 2) - 2 * div(u, 2) * rem(u, 2)

    @pl.loop(0, 16)
    def _(t):
        @pl.when(t == 3)
        def _():
            stage_2()

        @pl.when(t == 6)
        def _():
            stage_3()

        @pl.when(t == 8)
        def _():
            stage_4()

        dx, dz = gray(div(t, 4)), gray(rem(t, 4))
        at = column_at(dx, dz)

        @pl.when(t > 0)
        def _():
            arrived(part_of_sibling(kv, at, other), pair_recv.at[dx * 4 + dz])

        pltpu.make_async_copy(
            kv.at[:, pl.ds(at * 4, 4)], kv_out.at[:, pl.ds(at * 4, 4)], out_sem.at[t]
        ).start()
        v = kv[1, pl.ds(at * 4, 4)].reshape(COLUMN, D)
        attend(slice(None), query, keys_at(at), v, sums, total)

    row_sum = jnp.sum(sums[...], axis=1, keepdims=True)
    late_ref[...] = (total[...] / row_sum).astype(BF16).reshape(late_ref.shape)
    largest_ref[...] = jnp.full(largest_ref.shape, jnp.max(row_sum), F32)

    for make in sent:
        pltpu.make_async_remote_copy(*make(), device_id_type=MESH).wait_send()
    q_copy.wait()

    @pl.loop(0, 16)
    def _(t):
        at = column_at(gray(div(t, 4)), gray(rem(t, 4)))
        pltpu.make_async_copy(
            kv.at[:, pl.ds(at * 4, 4)], kv_out.at[:, pl.ds(at * 4, 4)], out_sem.at[t]
        ).wait()


def part_of_sibling(kv, at, other):
    return kv.at[:, pl.ds(at * 4, 4), other]


def gather(tokens, order, q, kv):
    slots = (2, SLOTS, 2, HALF, D)
    return pl.pallas_call(
        gather_kernel,
        out_shape=(
            jax.ShapeDtypeStruct((2, G, HALF, D), BF16),
            jax.ShapeDtypeStruct((8, D), F32),
            jax.ShapeDtypeStruct((4, G, HALF, D), BF16),
            jax.ShapeDtypeStruct(slots, BF16),
        ),
        in_specs=[
            pl.BlockSpec(memory_space=pltpu.SMEM),
            pl.BlockSpec(memory_space=pltpu.SMEM),
            pl.BlockSpec(memory_space=pl.ANY),
            pl.BlockSpec(memory_space=pl.ANY),
        ],
        out_specs=(
            pl.BlockSpec(memory_space=pltpu.VMEM),
            pl.BlockSpec(memory_space=pltpu.VMEM),
            pl.BlockSpec(memory_space=pl.ANY),
            pl.BlockSpec(memory_space=pl.ANY),
        ),
        scratch_shapes=[
            pltpu.VMEM(slots, BF16),
            pltpu.VMEM((TOKENS, D), BF16),
            pltpu.VMEM((4, G, HALF, D), BF16),
            pltpu.VMEM((LATE, 2 * D), BF16),
            pltpu.VMEM((LATE, D), F32),
            pltpu.VMEM((LATE, D), F32),
            pltpu.SemaphoreType.DMA((3,)),
            pltpu.SemaphoreType.DMA((16,)),
            pltpu.SemaphoreType.DMA((2, 3)),
            pltpu.SemaphoreType.DMA((2, 3)),
            pltpu.SemaphoreType.DMA((16, 4)),
            pltpu.SemaphoreType.DMA((16, 2)),
            pltpu.SemaphoreType.DMA((16,)),
            pltpu.SemaphoreType.DMA((16,)),
        ],
        compiler_params=pltpu.CompilerParams(
            collective_id=0, has_side_effects=True, vmem_limit_bytes=VMEM_LIMIT
        ),
        name="gather_and_late_rows",
    )(tokens, order, q, kv)


def early_kernel(
    tokens_ref,
    order_ref,
    late_ref,
    largest_ref,
    q_ref,
    kv_ref,
    out_ref,
    slot_at,
    keys,
    vals,
    query,
    total,
    sums,
    sem,
):
    x, y, z, core = place()
    column = 4 * x + z
    ends = stretch_ends(tokens_ref)

    @pl.loop(0, SLOTS)
    def _(slot):
        slot_at[order_ref[slot]] = slot

    def fetch(step, buffer):
        copies = []
        for i in range(4):
            slot = slot_at[step * 4 + i]
            copies.append(
                pltpu.make_async_copy(
                    kv_ref.at[0, slot], keys.at[buffer, pl.ds(2 * i, 2)], sem.at[buffer, i]
                )
            )
            copies.append(
                pltpu.make_async_copy(
                    kv_ref.at[1, slot], vals.at[buffer, pl.ds(2 * i, 2)], sem.at[buffer, 4 + i]
                )
            )
        return copies

    for copy in fetch(0, 0):
        copy.start()

    def visible_steps(block):
        last = block * SLOT + core * HALF + HALF - 1
        end = jnp.where(
            last < ends[0],
            ends[0],
            jnp.where(last < ends[1], ends[1], jnp.where(last < ends[2], ends[2], TOKENS)),
        )
        return div(end + COLUMN - 1, COLUMN)

    steps = []
    early_chip = []
    for pair in range(2):
        first = order_ref[column * 4 + 2 * pair]
        second = order_ref[column * 4 + 2 * pair + 1]
        chip = pair + 2 * (first > second).astype(jnp.int32)
        block = jnp.minimum(first, second)
        steps.append(visible_steps(block))
        early_chip.append(chip)
        extra = query_columns(block * SLOT + core * HALF, HALF, ends).astype(BF16)
        for g in range(G):
            rows = slice((pair * G + g) * HALF, (pair * G + g + 1) * HALF)
            query[rows, :D] = q_ref[chip, g]
            query[rows, D:] = extra

    total[...] = jnp.zeros_like(total)
    sums[...] = jnp.zeros_like(sums)

    def load(step, buffer):
        extra = key_columns(step * COLUMN, COLUMN, ends)
        k = jnp.concatenate([keys[buffer].reshape(COLUMN, D), extra], axis=1)
        return k, vals[buffer].reshape(COLUMN, D)

    for copy in fetch(0, 0):
        copy.wait()
    set_shift(query, load(0, 0)[0], LATE // 2)

    both = jnp.minimum(steps[0], steps[1])
    most = jnp.maximum(steps[0], steps[1])

    def next_step(step):
        @pl.when(step > 0)
        def _():
            for copy in fetch(step, rem(step, 2)):
                copy.wait()

        @pl.when(step + 1 < most)
        def _():
            for copy in fetch(step + 1, rem(step + 1, 2)):
                copy.start()

        return load(step, rem(step, 2))

    @pl.loop(0, both)
    def _(step):
        k, v = next_step(step)
        attend(slice(None), query, k, v, sums, total)

    first_row = (steps[1] > steps[0]).astype(jnp.int32) * (LATE // 2)

    @pl.loop(both, most)
    def _(step):
        k, v = next_step(step)
        attend(pl.ds(pl.multiple_of(first_row, LATE // 2), LATE // 2), query, k, v, sums, total)

    row_sum = jnp.sum(sums[...], axis=1, keepdims=True)
    early = (total[...] / row_sum).astype(BF16)
    for pair in range(2):
        chip = early_chip[pair]
        late_chip = 2 * pair + 2 - chip
        for g in range(G):
            rows = slice((pair * G + g) * HALF, (pair * G + g + 1) * HALF)
            out_ref[chip, :, g * D : (g + 1) * D] = early[rows]
            out_ref[late_chip, :, g * D : (g + 1) * D] = late_ref[pair, g]

    largest = jnp.maximum(jnp.max(row_sum), jnp.max(largest_ref[...]))

    @pl.when(jnp.logical_not(largest < TOO_LARGE))
    def _():
        for chip in range(4):
            slot = column * 4 + 2 * (chip % 2) + chip // 2
            block = order_ref[slot]
            for g in range(G):
                query[:HALF, :D] = q_ref[chip, g]
                query[:HALF, D:] = query_columns(block * SLOT + core * HALF, HALF, ends).astype(BF16)
                total[:HALF, :] = jnp.zeros((HALF, D), F32)
                sums[:HALF, :] = jnp.zeros((HALF, D), F32)
                sums[HALF : 2 * HALF, :] = jnp.full((HALF, D), -1e30, F32)

                @pl.loop(0, visible_steps(block))
                def _(step):
                    for copy in fetch(step, 0):
                        copy.start()
                    for copy in fetch(step, 0):
                        copy.wait()
                    k, v = load(step, 0)
                    scores = scores_of(query[:HALF, :], k) * TO_LOG2
                    old = sums[HALF : 2 * HALF, :]
                    new = jnp.maximum(old, jnp.max(scores, axis=1, keepdims=True))
                    factor = jnp.exp2(old - new)
                    weights = jnp.exp2(scores - new[:, :1])
                    sums[HALF : 2 * HALF, :] = new
                    sums[:HALF, :] = sums[:HALF, :] * factor + lane_sum(weights)
                    total[:HALF, :] = total[:HALF, :] * factor + jnp.dot(
                        weights.astype(BF16), v, preferred_element_type=F32
                    )

                row_sum = jnp.sum(sums[:HALF, :], axis=1, keepdims=True)
                out_ref[chip, :, g * D : (g + 1) * D] = (total[:HALF, :] / row_sum).astype(BF16)


def early_rows(tokens, order, late, largest, q, kv):
    return pl.pallas_call(
        early_kernel,
        out_shape=jax.ShapeDtypeStruct((4, HALF, G * D), BF16),
        in_specs=[
            pl.BlockSpec(memory_space=pltpu.SMEM),
            pl.BlockSpec(memory_space=pltpu.SMEM),
            pl.BlockSpec(memory_space=pltpu.VMEM),
            pl.BlockSpec(memory_space=pltpu.VMEM),
            pl.BlockSpec(memory_space=pltpu.VMEM),
            pl.BlockSpec(memory_space=pl.ANY),
        ],
        out_specs=pl.BlockSpec(memory_space=pltpu.VMEM),
        scratch_shapes=[
            pltpu.SMEM((SLOTS,), jnp.int32),
            pltpu.VMEM((2, 8, HALF, D), BF16),
            pltpu.VMEM((2, 8, HALF, D), BF16),
            pltpu.VMEM((LATE, 2 * D), BF16),
            pltpu.VMEM((LATE, D), F32),
            pltpu.VMEM((LATE, D), F32),
            pltpu.SemaphoreType.DMA((2, 8)),
        ],
        compiler_params=pltpu.CompilerParams(vmem_limit_bytes=VMEM_LIMIT),
        name="early_rows",
    )(tokens, order, late, largest, q, kv)


def return_kernel(in_ref, out_ref, send_sem, recv_sem, local_sem):
    x, y, z, core = place()
    line = [device_at(x, rem(y + d, 4), z, core) for d in (1, 2, 3)]
    barrier = pltpu.get_barrier_semaphore()
    for partner in line:
        pl.semaphore_signal(barrier, inc=1, device_id=partner, device_id_type=MESH)
    pl.semaphore_wait(barrier, 3)
    lanes = pl.ds(pl.multiple_of(y * (G * D), D), G * D)
    copies = []
    for d in (1, 3, 2):
        copy = pltpu.make_async_remote_copy(
            src_ref=in_ref.at[rem(y + d, 4)],
            dst_ref=out_ref.at[:, lanes],
            send_sem=send_sem.at[d - 1],
            recv_sem=recv_sem.at[d - 1],
            device_id=line[d - 1],
            device_id_type=MESH,
        )
        copy.start()
        copies.append(copy)
    own = pltpu.make_async_copy(in_ref.at[y], out_ref.at[:, lanes], local_sem)
    own.start()
    own.wait()
    for d in (1, 3, 2):
        lanes = pl.ds(pl.multiple_of((rem(y + 4 - d, 4)) * (G * D), D), G * D)
        there = out_ref.at[:, lanes]
        pltpu.make_async_copy(there, there, recv_sem.at[d - 1]).wait()
    for copy in copies:
        copy.wait_send()


def return_rows(attended):
    return pl.pallas_call(
        return_kernel,
        out_shape=jax.ShapeDtypeStruct((HALF, 4 * G * D), BF16),
        in_specs=[pl.BlockSpec(memory_space=pltpu.VMEM)],
        out_specs=pl.BlockSpec(memory_space=pltpu.VMEM),
        scratch_shapes=[
            pltpu.SemaphoreType.DMA((3,)),
            pltpu.SemaphoreType.DMA((3,)),
            pltpu.SemaphoreType.DMA,
        ],
        compiler_params=pltpu.CompilerParams(collective_id=1, has_side_effects=True),
        name="return_rows",
    )(attended)


def body(queries, keys, values, stretch_tokens, block_order):
    q = jnp.transpose(queries, (1, 0, 2))
    kv = jnp.stack([jnp.transpose(keys, (1, 0, 2)), jnp.transpose(values, (1, 0, 2))], axis=1)
    late, largest, q_all, kv_all = gather(stretch_tokens, block_order, q, kv)
    attended = early_rows(stretch_tokens, block_order, late, largest, q_all, kv_all)
    return return_rows(attended)


def solution(mesh):
    return jax.shard_map(
        body,
        mesh=mesh,
        in_specs=(
            P(("ctx", "uly"), None, None),
            P(("ctx", "uly"), None, None),
            P(("ctx", "uly"), None, None),
            P(),
            P(),
        ),
        out_specs=P(("ctx", "uly"), None),
        check_vma=False,
    )
```

```python
import math

import jax
import jax.numpy as jnp
from jax import lax
from jax.experimental import pallas as pl
from jax.experimental.pallas import tpu as pltpu
from jax.sharding import PartitionSpec as P

MESH = pl.DeviceIdType.MESH
F32 = jnp.float32
BF16 = jnp.bfloat16

D = 128
G = 6
HALF = 128
SLOTS = 64
SLOT = 256
COLUMN = 1024
ROWS = G * HALF
TOKENS = SLOTS * SLOT
TO_LOG2 = (D**-0.5) * 1.4426950408889634
HIDDEN = -30000.0
SAFE_LOG2 = 90.0
VMEM_LIMIT = 60 * 2**20


def div(a, n):
    return lax.div(a, n)


def rem(a, n):
    return lax.rem(a, n)


def place():
    ctx, uly = lax.axis_index("ctx"), lax.axis_index("uly")
    return div(ctx, 8), div(uly, 2) * 2 + rem(ctx, 2), rem(div(ctx, 2), 4), rem(uly, 2)


def device_at(x, y, z, core):
    return (x * 8 + z * 2 + rem(y, 2), div(y, 2) * 2 + core)


def slot_in_column(chip):
    return 2 * rem(chip, 2) + div(chip, 2)


def stretch_ends(tokens_ref):
    first = tokens_ref[0]
    second = first + tokens_ref[1]
    return first, second, second + tokens_ref[2]


def stretch_of(position, ends):
    total = (position >= ends[0]).astype(jnp.int32)
    for end in ends[1:]:
        total = total + (position >= end).astype(jnp.int32)
    return total


def key_columns(first_position, rows, ends):
    position = first_position + lax.broadcasted_iota(jnp.int32, (rows, D), 0)
    lane = lax.broadcasted_iota(jnp.int32, (rows, D), 1)
    return jnp.where(lane < stretch_of(position, ends), HIDDEN, 0.0).astype(BF16)


def query_columns(first_position, rows, ends):
    position = first_position + lax.broadcasted_iota(jnp.int32, (rows, D), 0)
    lane = lax.broadcasted_iota(jnp.int32, (rows, D), 1)
    return jnp.where(lane == stretch_of(position, ends), 1.0, 0.0).astype(BF16)


def lane_sum(x):
    total = x[:, :D]
    for j in range(1, x.shape[1] // D):
        total = total + x[:, j * D : (j + 1) * D]
    return total


def largest_square(x):
    x = x.reshape(-1, D).astype(F32)
    return jnp.max(jnp.sum(x * x, axis=1, keepdims=True))


def scores_of(q, k):
    return lax.dot_general(q, k, (((1,), (1,)), ((), ())), preferred_element_type=F32)


def attention_kernel(
    tokens_ref,
    order_ref,
    q_ref,
    kv_ref,
    out_ref,
    safe_ref,
    kv,
    columns,
    query,
    marks,
    total,
    sums,
    finished,
    local_sem,
    line_send,
    line_recv,
    ring_send,
    ring_recv,
    pair_send,
    pair_recv,
    back_send,
    back_recv,
    norms,
    norm_send,
    norm_recv,
):
    x, y, z, core = place()
    other = 1 - core
    column = 4 * x + z
    ends = stretch_ends(tokens_ref)

    def column_at(dx, dz):
        return rem(x + dx, 4) * 4 + rem(z + dz, 4)

    def along(da, db):
        return da * (1 - core) + db * core, da * core + db * (1 - core)

    def chunk(da, db):
        return column_at(*along(da, db)) * 4

    def device_along(da, db):
        dx, dz = along(da, db)
        return device_at(rem(x + dx, 4), y, rem(z + dz, 4), core)

    line = [device_at(x, rem(y + d, 4), z, core) for d in (1, 2, 3)]
    ring = [device_along(*o) for o in ((1, 0), (3, 0), (0, 1), (0, 3))]
    sibling = device_at(x, y, z, other)

    barrier = pltpu.get_barrier_semaphore()
    across = [device_at(rem(x + 2, 4), y, z, core), device_at(x, y, rem(z + 2, 4), core)]
    for partner in (*line, *ring, sibling, *across):
        pl.semaphore_signal(barrier, inc=1, device_id=partner, device_id_type=MESH)
    pl.semaphore_wait(barrier, 10)

    sent = []

    def send(make):
        pltpu.make_async_remote_copy(*make(), device_id_type=MESH).start()
        sent.append(make)

    own_slot = column * 4 + slot_in_column(y)
    for d in (1, 3, 2):
        send(
            lambda d=d: (
                kv_ref.at[rem(y + d, 4)],
                kv.at[:, own_slot, core],
                line_send.at[0, d - 1],
                line_recv.at[0, d - 1],
                line[d - 1],
            )
        )
    own_kv = pltpu.make_async_copy(kv_ref.at[y], kv.at[:, own_slot, core], local_sem.at[0])
    own_kv.start()
    def send_query(d):
        send(
            lambda: (
                q_ref.at[pl.ds(G * rem(y + d, 4), G)],
                query.at[4 - d],
                line_send.at[1, d - 1],
                line_recv.at[1, d - 1],
                line[d - 1],
            )
        )

    own_q = pltpu.make_async_copy(q_ref.at[pl.ds(G * y, G)], query.at[0], local_sem.at[1])
    own_q.start()

    def arrived(dst, sem):
        pltpu.make_async_copy(dst, dst, sem).wait()

    def part(da, db):
        return kv.at[:, pl.ds(chunk(da, db), 4), core]

    def hop(da, db, step_a, step_b):
        there = (da - step_a) % 4 * 4 + (db - step_b) % 4

        def make():
            src = part(da, db)
            return (
                src,
                src,
                ring_send.at[da * 4 + db, step_a if step_a else 3 + step_b],
                ring_recv.at[there],
                device_along(step_a, step_b),
            )

        send(make)

    def near_a():
        hop(0, 0, 1, 0)
        hop(0, 0, 3, 0)

    def near_b(da):
        hop(da, 0, 0, 1)
        hop(da, 0, 0, 3)

    def far_b(da):
        hop(da, 0, 0, 2)

    def take(da, db):
        arrived(part(da, db), ring_recv.at[da * 4 + db])

    def share(da, db):
        def make():
            dx, dz = along(da, db)
            src = part(da, db)
            at = dx * 4 + dz
            return src, src, pair_send.at[at], pair_recv.at[at], sibling

        send(make)

    def take_and_share(*offsets):
        for offset in offsets:
            take(*offset)
            share(*offset)

    def stage_0():
        near_a()
        near_b(0)
        share(0, 0)

    def stage_1():
        take(1, 0)
        take(3, 0)
        hop(0, 0, 2, 0)
        near_b(1)
        near_b(3)
        share(1, 0)
        share(3, 0)
        take_and_share((0, 1), (0, 3))

    def stage_2():
        take_and_share((1, 1), (1, 3), (3, 1), (3, 3))
        for da in (0, 1, 3):
            far_b(da)

    def stage_3():
        take(2, 0)
        near_b(2)
        far_b(2)
        share(2, 0)

    def stage_4():
        take_and_share((0, 2), (1, 2), (3, 2))

    def stage_5():
        take_and_share((2, 1), (2, 3), (2, 2))

    @pl.loop(0, SLOTS)
    def _(slot):
        rows = pl.ds(pl.multiple_of(slot * SLOT, SLOT), SLOT)
        columns[rows, :] = key_columns(order_ref[slot] * SLOT, SLOT, ends)

    send_query(1)
    send_query(3)

    for d in (1, 3, 2):
        from_slot = column * 4 + slot_in_column(rem(y + 4 - d, 4))
        arrived(kv.at[:, from_slot, core], line_recv.at[0, d - 1])
    own_kv.wait()
    send_query(2)
    stage_0()

    for d in range(4):
        slot = column * 4 + slot_in_column(rem(y + d, 4))
        marks[d] = query_columns(order_ref[slot] * SLOT + core * HALF, HALF, ends)
    total[...] = jnp.zeros_like(total)
    sums[...] = jnp.zeros_like(sums)

    def attend(block, blocks, at, count):
        k = kv[0, pl.ds(at * 4, 4 * count)].reshape(count * COLUMN, D)
        v = kv[1, pl.ds(at * 4, 4 * count)].reshape(count * COLUMN, D)
        start = pl.multiple_of(at * COLUMN, COLUMN)
        k = jnp.concatenate([k, columns[pl.ds(start, count * COLUMN), :]], axis=1)
        here = pl.ds(block, blocks)
        q = query[here].reshape(blocks * ROWS, D)
        mark = jnp.broadcast_to(marks[here][:, None], (blocks, G, HALF, D))
        q = jnp.concatenate([q, mark.reshape(blocks * ROWS, D)], axis=1)
        weights = jnp.exp2(scores_of(q, k) * TO_LOG2)
        sums[here] += lane_sum(weights).reshape(blocks, ROWS, D)
        product = jnp.dot(weights.astype(BF16), v, preferred_element_type=F32)
        total[here] += product.reshape(blocks, ROWS, D)

    own_q.wait()
    arrived(part_of_sibling(kv, column, other), pair_recv.at[0])

    def take_query(d):
        arrived(query.at[d], line_recv.at[1, 3 - d])

    @pl.loop(0, 4)
    def _(t):
        block = t + div(t, 2) - 2 * div(t, 3)

        @pl.when(t == 1)
        def _():
            take_query(1)
            take_query(3)

        @pl.when(t == 3)
        def _():
            stage_1()
            take_query(2)

        attend(block, 1, column, 1)

    stages = (
        line,
        [device_at(rem(x + d, 4), y, z, core) for d in (1, 2, 3)],
        [device_at(x, y, rem(z + d, 4), core) for d in (1, 2, 3)],
        [sibling],
    )

    def norms_start(stage):
        for i, device in enumerate(stages[stage]):
            send(
                lambda i=i, device=device: (
                    norms.at[stage, 0],
                    norms.at[stage, 1 + i],
                    norm_send.at[stage, i],
                    norm_recv.at[stage, i],
                    device,
                )
            )

    def norms_end(stage):
        largest = norms[stage, 0]
        for i in range(len(stages[stage])):
            arrived(norms.at[stage, 1 + i], norm_recv.at[stage, i])
            largest = jnp.maximum(largest, norms[stage, 1 + i])
        if stage < 3:
            norms[stage + 1, 0] = largest
        else:
            safe = (largest[0, 0] * largest[4, 0] < (SAFE_LOG2 / TO_LOG2) ** 2).astype(jnp.int32)
            safe_ref[0] = safe

    q_square = largest_square(query[...])
    k_square = largest_square(kv[0, pl.ds(column * 4, 4)])
    upper = lax.broadcasted_iota(jnp.int32, (8, D), 0) < 4
    norms[0, 0] = jnp.where(upper, q_square, k_square)
    norms_start(0)

    @pl.loop(0, 11)
    def _(t):
        for when, stage in ((3, stage_2), (4, stage_3), (7, stage_4), (9, stage_5)):

            @pl.when(t == when)
            def _():
                stage()

        for stage in range(4):

            @pl.when(t == 2 + 2 * stage)
            def _():
                norms_end(stage)
                if stage < 3:
                    norms_start(stage + 1)

        u, v = div(t, 4), rem(t, 4)
        a, b = div(v, 2), 1 + 2 * rem(v, 2)
        is_0, is_1, is_2 = div((1 - u) * (2 - u), 2), u * (2 - u), div(u * (u - 1), 2)
        dx = is_0 * a * b + is_1 * (1 + 2 * a) + is_2 * (v + a)
        dz = is_0 * (1 - a) * b + is_1 * b + is_2 * 2
        at = column_at(dx, dz)
        arrived(part_of_sibling(kv, at, other), pair_recv.at[dx * 4 + dz])
        attend(0, 4, at, 1)

    for dz in range(4):
        arrived(part_of_sibling(kv, column_at(2, dz), other), pair_recv.at[8 + dz])

    def back(d):
        lanes = pl.ds(pl.multiple_of(y * ROWS, ROWS), ROWS)
        return (
            finished.at[d],
            out_ref.at[:, lanes],
            back_send.at[d - 1],
            back_recv.at[d - 1],
            line[d - 1],
        )

    @pl.loop(0, 4)
    def _(t):
        block = 2 - t + 3 * div(t, 2) - 2 * div(t, 3)
        attend(block, 1, rem(x + 2, 4) * 4, 4)
        row_sum = jnp.sum(sums[block], axis=1, keepdims=True)
        attended = (total[block] / row_sum).astype(BF16)
        for g in range(G):
            finished[block, :, g * D : (g + 1) * D] = attended[g * HALF : (g + 1) * HALF]
        for i, d in enumerate((2, 1, 3)):

            @pl.when(t == i)
            def _():
                send(lambda d=d: back(d))

    lanes = pl.ds(pl.multiple_of(y * ROWS, ROWS), ROWS)
    own = pltpu.make_async_copy(finished.at[0], out_ref.at[:, lanes], local_sem.at[0])
    own.start()
    for make in sent:
        pltpu.make_async_remote_copy(*make(), device_id_type=MESH).wait_send()
    own.wait()
    for d in (2, 1, 3):
        lanes = pl.ds(pl.multiple_of(rem(y + 4 - d, 4) * ROWS, ROWS), ROWS)
        arrived(out_ref.at[:, lanes], back_recv.at[d - 1])


def part_of_sibling(kv, at, other):
    return kv.at[:, pl.ds(at * 4, 4), other]


def attention(tokens, order, q, kv):
    return pl.pallas_call(
        attention_kernel,
        out_shape=(
            jax.ShapeDtypeStruct((HALF, 4 * ROWS), BF16),
            jax.ShapeDtypeStruct((1,), jnp.int32),
        ),
        in_specs=[
            pl.BlockSpec(memory_space=pltpu.SMEM),
            pl.BlockSpec(memory_space=pltpu.SMEM),
            pl.BlockSpec(memory_space=pl.ANY),
            pl.BlockSpec(memory_space=pl.ANY),
        ],
        out_specs=(
            pl.BlockSpec(memory_space=pltpu.VMEM),
            pl.BlockSpec(memory_space=pltpu.SMEM),
        ),
        scratch_shapes=[
            pltpu.VMEM((2, SLOTS, 2, HALF, D), BF16),
            pltpu.VMEM((TOKENS, D), BF16),
            pltpu.VMEM((4, G, HALF, D), BF16),
            pltpu.VMEM((4, HALF, D), BF16),
            pltpu.VMEM((4, ROWS, D), F32),
            pltpu.VMEM((4, ROWS, D), F32),
            pltpu.VMEM((4, HALF, ROWS), BF16),
            pltpu.SemaphoreType.DMA((2,)),
            pltpu.SemaphoreType.DMA((2, 3)),
            pltpu.SemaphoreType.DMA((2, 3)),
            pltpu.SemaphoreType.DMA((16, 7)),
            pltpu.SemaphoreType.DMA((16,)),
            pltpu.SemaphoreType.DMA((16,)),
            pltpu.SemaphoreType.DMA((16,)),
            pltpu.SemaphoreType.DMA((3,)),
            pltpu.SemaphoreType.DMA((3,)),
            pltpu.VMEM((4, 4, 8, D), F32),
            pltpu.SemaphoreType.DMA((4, 3)),
            pltpu.SemaphoreType.DMA((4, 3)),
        ],
        compiler_params=pltpu.CompilerParams(
            collective_id=0, has_side_effects=True, vmem_limit_bytes=VMEM_LIMIT
        ),
        name="attention",
    )(tokens, order, q, kv)


negative = -1e30


def stretch_lookup(positions, stretch_ends):
    return jnp.sum((stretch_ends[None, :] <= positions[:, None]).astype(jnp.int32), axis=1)


def row_stretches(first_row, piece_rows, block_order, stretch_ends, block_rows):
    row_ids = first_row + jnp.arange(piece_rows, dtype=jnp.int32)
    slot_index = row_ids // block_rows
    slot_ids = jnp.arange(block_order.shape[0], dtype=jnp.int32)
    owners = jnp.sum(
        jnp.where(slot_index[:, None] == slot_ids[None, :], block_order[None, :], 0), axis=1
    )
    return stretch_lookup(owners * block_rows + row_ids % block_rows, stretch_ends)


def attend_tile(
    partial_value, query_part, query_stretch, key_part, value_part, key_stretch, score_scale
):
    run_max, run_sum, numerator = partial_value
    scores = (
        jnp.einsum("qhgd,khd->hgqk", query_part, key_part, preferred_element_type=jnp.float32)
        * score_scale
    )
    visible = key_stretch[None, :] <= query_stretch[:, None]
    masked = jnp.where(visible, scores, negative)
    new_max = jnp.maximum(run_max, jnp.max(masked, axis=-1))
    weights = jnp.where(visible, jnp.exp(masked - new_max[..., None]), 0.0)
    factor = jnp.exp(run_max - new_max)
    new_sum = run_sum * factor + jnp.sum(weights, axis=-1)
    product = jnp.einsum(
        "hgqk,khd->qhgd",
        weights.astype(jnp.bfloat16),
        value_part,
        preferred_element_type=jnp.float32,
    )
    new_numerator = numerator * jnp.transpose(factor, (2, 0, 1))[..., None] + product
    return (new_max, new_sum, new_numerator)


def empty_partial(length, kv_local, group_size, head_dim):
    return (
        jnp.full((kv_local, group_size, length), negative, jnp.float32),
        jnp.zeros((kv_local, group_size, length), jnp.float32),
        jnp.zeros((length, kv_local, group_size, head_dim), jnp.float32),
    )


def everywhere(x):
    copies = jnp.broadcast_to(x[None], (lax.axis_size("ctx"), *x.shape))
    return lax.all_to_all(copies, "ctx", split_axis=0, concat_axis=0).reshape(-1, *x.shape[1:])


def shifted_body(queries, keys, values, stretch_tokens, block_order):
    tok_rows, heads_query, head_dim = queries.shape
    heads_kv = keys.shape[1]
    group_size = heads_query // heads_kv
    uly_size = lax.axis_size("uly")
    row_count = tok_rows * uly_size
    block_rows = row_count // 2
    kv_local = heads_kv // uly_size
    score_scale = head_dim ** (-0.5)
    stretch_ends = jnp.cumsum(stretch_tokens)
    ctx_index = lax.axis_index("ctx")
    query_stretch = row_stretches(
        ctx_index * row_count, row_count, block_order, stretch_ends, block_rows
    )
    query_local, key_local, value_local = (
        lax.all_to_all(queries, "uly", split_axis=1, concat_axis=0, tiled=True),
        lax.all_to_all(keys, "uly", split_axis=1, concat_axis=0, tiled=True),
        lax.all_to_all(values, "uly", split_axis=1, concat_axis=0, tiled=True),
    )
    query_local = query_local.reshape(row_count, kv_local, group_size, head_dim)
    query_spans = ((0, row_count),)
    initial = tuple(
        (empty_partial(length, kv_local, group_size, head_dim) for offset, length in query_spans)
    )
    key_piece = everywhere(key_local)
    piece_rows = key_piece.shape[0]
    key_stretches = row_stretches(jnp.int32(0), piece_rows, block_order, stretch_ends, block_rows)
    tile_rows = math.gcd(piece_rows, 1024)
    tile_count = piece_rows // tile_rows
    stacked = (
        key_piece.reshape(tile_count, tile_rows, kv_local, head_dim),
        everywhere(value_local).reshape(
            tile_count, tile_rows, kv_local, head_dim
        ),
        key_stretches.reshape(tile_count, tile_rows),
    )

    def one_tile(partials, tile_parts):
        key_part, value_part, key_stretch = tile_parts
        updated = []
        for (offset, length), partial_value in zip(query_spans, partials):
            partial_value = attend_tile(
                partial_value,
                query_local,
                query_stretch,
                key_part,
                value_part,
                key_stretch,
                score_scale,
            )
            updated.append(partial_value)
        return (tuple(updated), None)

    result, unused = lax.scan(one_tile, initial, stacked)
    partials = result
    outputs = []
    for partial_value in partials:
        run_max, run_sum, numerator = partial_value
        outputs.append(numerator / jnp.transpose(run_sum, (2, 0, 1))[..., None])
    attended = outputs[0].astype(jnp.bfloat16)
    attended = attended.reshape(row_count, heads_query // uly_size, head_dim)
    returned = lax.all_to_all(attended, "uly", split_axis=0, concat_axis=1, tiled=True)
    return returned.reshape(tok_rows, heads_query * head_dim)


def body(queries, keys, values, stretch_tokens, block_order):
    q = jnp.transpose(queries, (1, 0, 2))
    kv = jnp.stack([jnp.transpose(keys, (1, 0, 2)), jnp.transpose(values, (1, 0, 2))], axis=1)
    attended, safe = attention(stretch_tokens, block_order, q, kv)
    return lax.cond(
        safe[0] == 1,
        lambda: attended,
        lambda: shifted_body(queries, keys, values, stretch_tokens, block_order),
    )


def solution(mesh):
    return jax.shard_map(
        body,
        mesh=mesh,
        in_specs=(
            P(("ctx", "uly"), None, None),
            P(("ctx", "uly"), None, None),
            P(("ctx", "uly"), None, None),
            P(),
            P(),
        ),
        out_specs=P(("ctx", "uly"), None),
        check_vma=False,
    )
```

```python
import math

import jax
import jax.numpy as jnp
from jax import lax
from jax.experimental import pallas as pl
from jax.experimental.pallas import tpu as pltpu
from jax.sharding import PartitionSpec as P

MESH = pl.DeviceIdType.MESH
F32 = jnp.float32
BF16 = jnp.bfloat16

D = 128
G = 6
HALF = 128
SLOTS = 64
SLOT = 256
COLUMN = 1024
ROWS = G * HALF
TOKENS = SLOTS * SLOT
TO_LOG2 = (D**-0.5) * 1.4426950408889634
HIDDEN = -30000.0
SAFE_LOG2 = 90.0
VMEM_LIMIT = 60 * 2**20


def div(a, n):
    return lax.div(a, n)


def rem(a, n):
    return lax.rem(a, n)


def place():
    ctx, uly = lax.axis_index("ctx"), lax.axis_index("uly")
    return div(ctx, 8), div(uly, 2) * 2 + rem(ctx, 2), rem(div(ctx, 2), 4), rem(uly, 2)


def device_at(x, y, z, core):
    return (x * 8 + z * 2 + rem(y, 2), div(y, 2) * 2 + core)


def slot_in_column(chip):
    return 2 * rem(chip, 2) + div(chip, 2)


def stretch_ends(tokens_ref):
    first = tokens_ref[0]
    second = first + tokens_ref[1]
    return first, second, second + tokens_ref[2]


def stretch_of(position, ends):
    total = (position >= ends[0]).astype(jnp.int32)
    for end in ends[1:]:
        total = total + (position >= end).astype(jnp.int32)
    return total


def key_columns(first_position, rows, ends):
    position = first_position + lax.broadcasted_iota(jnp.int32, (rows, D), 0)
    lane = lax.broadcasted_iota(jnp.int32, (rows, D), 1)
    return jnp.where(lane < stretch_of(position, ends), HIDDEN, 0.0).astype(BF16)


def query_columns(first_position, rows, ends):
    position = first_position + lax.broadcasted_iota(jnp.int32, (rows, D), 0)
    lane = lax.broadcasted_iota(jnp.int32, (rows, D), 1)
    return jnp.where(lane == stretch_of(position, ends), 1.0, 0.0).astype(BF16)


def lane_sum(x):
    total = x[:, :D]
    for j in range(1, x.shape[1] // D):
        total = total + x[:, j * D : (j + 1) * D]
    return total


def largest_square(x):
    x = x.reshape(-1, D).astype(F32)
    return jnp.max(jnp.sum(x * x, axis=1, keepdims=True))


def scores_of(q, k):
    return lax.dot_general(q, k, (((1,), (1,)), ((), ())), preferred_element_type=F32)


def attention_kernel(
    tokens_ref,
    order_ref,
    q_in,
    k_in,
    v_in,
    out_ref,
    safe_ref,
    q_ref,
    kv_ref,
    kv,
    columns,
    query,
    marks,
    total,
    sums,
    finished,
    local_sem,
    line_send,
    line_recv,
    ring_send,
    ring_recv,
    pair_send,
    pair_recv,
    back_send,
    back_recv,
    norms,
    norm_send,
    norm_recv,
):
    x, y, z, core = place()
    other = 1 - core
    column = 4 * x + z
    ends = stretch_ends(tokens_ref)

    def column_at(dx, dz):
        return rem(x + dx, 4) * 4 + rem(z + dz, 4)

    a_step = [4 * (rem(x + d, 4) - x) * (1 - core) + (rem(z + d, 4) - z) * core for d in range(4)]
    b_step = [4 * (rem(x + d, 4) - x) * core + (rem(z + d, 4) - z) * (1 - core) for d in range(4)]

    def along(da, db):
        return da * (1 - core) + db * core, da * core + db * (1 - core)

    def chunk(da, db):
        return column + a_step[da] + b_step[db]

    y_low, here_uly = rem(y, 2), div(y, 2) * 2 + core

    def device_along(da, db):
        return (2 * chunk(da, db) + y_low, here_uly)

    line = [device_at(x, rem(y + d, 4), z, core) for d in (1, 2, 3)]
    ring = [device_along(*o) for o in ((1, 0), (3, 0), (0, 1), (0, 3))]
    sibling = device_at(x, y, z, other)

    barrier = pltpu.get_barrier_semaphore()
    across = [device_at(rem(x + 2, 4), y, z, core), device_at(x, y, rem(z + 2, 4), core)]
    for partner in (*line, *ring, sibling, *across):
        pl.semaphore_signal(barrier, inc=1, device_id=partner, device_id_type=MESH)
    kv_ref[:, 0] = jnp.swapaxes(k_in[...], 0, 1)
    kv_ref[:, 1] = jnp.swapaxes(v_in[...], 0, 1)
    q_ref[...] = jnp.swapaxes(q_in[...], 0, 1)
    upper = lax.broadcasted_iota(jnp.int32, (8, D), 0) < 4
    norms[0, 0] = jnp.where(upper, largest_square(q_in[...]), largest_square(k_in[...]))
    pl.semaphore_wait(barrier, 10)

    sent = []

    def send(make):
        pltpu.make_async_remote_copy(*make(), device_id_type=MESH).start()
        sent.append(make)

    stages = (
        [device_at(rem(x + d, 4), y, z, core) for d in (1, 2, 3)],
        [device_at(x, y, rem(z + d, 4), core) for d in (1, 2, 3)],
        [sibling],
        line,
    )

    def norms_start(stage):
        for i, device in enumerate(stages[stage]):
            send(
                lambda i=i, device=device: (
                    norms.at[stage, 0],
                    norms.at[stage, 1 + i],
                    norm_send.at[stage, i],
                    norm_recv.at[stage, i],
                    device,
                )
            )

    def norms_end(stage):
        largest = norms[stage, 0]
        for i in range(len(stages[stage])):
            arrived(norms.at[stage, 1 + i], norm_recv.at[stage, i])
            largest = jnp.maximum(largest, norms[stage, 1 + i])
        if stage < 3:
            norms[stage + 1, 0] = largest
        else:
            safe = (largest[0, 0] * largest[4, 0] < (SAFE_LOG2 / TO_LOG2) ** 2).astype(jnp.int32)
            safe_ref[0] = safe

    norms_start(0)

    def slab(chip):
        rows = pl.ds(pl.multiple_of(slot_in_column(chip) * HALF, HALF), HALF)
        return kv.at[column, core, :, rows]

    ys = [y] + [rem(y + d, 4) for d in (1, 2, 3)]
    for d in (1, 3, 2):
        send(
            lambda d=d: (
                kv_ref.at[ys[d]],
                slab(y),
                line_send.at[0, d - 1],
                line_recv.at[0, d - 1],
                line[d - 1],
            )
        )
    own_kv = pltpu.make_async_copy(kv_ref.at[y], slab(y), local_sem.at[0])
    own_kv.start()
    def send_query(d):
        send(
            lambda: (
                q_ref.at[pl.ds(G * ys[d], G)],
                query.at[4 - d],
                line_send.at[1, d - 1],
                line_recv.at[1, d - 1],
                line[d - 1],
            )
        )

    own_q = pltpu.make_async_copy(q_ref.at[pl.ds(G * y, G)], query.at[0], local_sem.at[1])
    own_q.start()

    def arrived(dst, sem):
        pltpu.make_async_copy(dst, dst, sem).wait()

    def part(da, db):
        return kv.at[chunk(da, db), core]

    def hop(da, db, step_a, step_b):
        there = (da - step_a) % 4 * 4 + (db - step_b) % 4

        def make():
            src = part(da, db)
            return (
                src,
                src,
                ring_send.at[da * 4 + db, step_a if step_a else 3 + step_b],
                ring_recv.at[there],
                device_along(step_a, step_b),
            )

        send(make)

    def near_a():
        hop(0, 0, 1, 0)
        hop(0, 0, 3, 0)

    def near_b(da):
        hop(da, 0, 0, 1)
        hop(da, 0, 0, 3)

    def far_b(da):
        hop(da, 0, 0, 2)

    def take(da, db):
        arrived(part(da, db), ring_recv.at[da * 4 + db])

    def share(da, db):
        def make():
            dx, dz = along(da, db)
            src = part(da, db)
            at = dx * 4 + dz
            return src, src, pair_send.at[at], pair_recv.at[at], sibling

        send(make)

    def take_and_share(*offsets):
        for offset in offsets:
            take(*offset)
            share(*offset)

    def stage_0():
        near_a()
        near_b(0)
        share(0, 0)

    def stage_1():
        take(1, 0)
        take(3, 0)
        hop(0, 0, 2, 0)
        near_b(1)
        near_b(3)
        share(1, 0)
        share(3, 0)
        take_and_share((0, 1), (0, 3))

    def stage_2():
        take_and_share((1, 1), (1, 3), (3, 1), (3, 3))
        for da in (0, 1, 3):
            far_b(da)

    def stage_3():
        take(2, 0)
        near_b(2)
        far_b(2)
        share(2, 0)

    def stage_4():
        take_and_share((0, 2), (1, 2), (3, 2))

    def stage_5():
        take_and_share((2, 1), (2, 3), (2, 2))

    @pl.loop(0, 16)
    def _(at):
        for j in range(4):
            extra = key_columns(order_ref[at * 4 + j] * SLOT, SLOT, ends)
            for half in range(2):
                rows = slice(j * HALF, (j + 1) * HALF)
                columns[at, half, rows] = extra[half * HALF : (half + 1) * HALF]

    send_query(1)
    send_query(3)

    for d in (1, 3, 2):
        arrived(slab(ys[4 - d]), line_recv.at[0, d - 1])
    own_kv.wait()
    norms_end(0)
    norms_start(1)
    send_query(2)
    stage_0()

    for d in range(4):
        slot = column * 4 + slot_in_column(rem(y + d, 4))
        marks[d] = query_columns(order_ref[slot] * SLOT + core * HALF, HALF, ends)
    total[...] = jnp.zeros_like(total)
    sums[...] = jnp.zeros_like(sums)

    def attend(block, blocks, at, count):
        there = pl.ds(at, count)
        k = kv[there, :, 0].reshape(count * COLUMN, D)
        v = kv[there, :, 1].reshape(count * COLUMN, D)
        extra = columns[there].reshape(count * COLUMN, D)
        k = jnp.concatenate([k, extra], axis=1)
        here = pl.ds(block, blocks)
        q = query[here].reshape(blocks * ROWS, D)
        mark = jnp.broadcast_to(marks[here][:, None], (blocks, G, HALF, D))
        q = jnp.concatenate([q, mark.reshape(blocks * ROWS, D)], axis=1)
        weights = jnp.exp2(scores_of(q, k) * TO_LOG2)
        sums[here] += lane_sum(weights).reshape(blocks, ROWS, D)
        product = jnp.dot(weights.astype(BF16), v, preferred_element_type=F32)
        total[here] += product.reshape(blocks, ROWS, D)

    own_q.wait()
    arrived(part_of_sibling(kv, column, other), pair_recv.at[0])

    def take_query(d):
        arrived(query.at[d], line_recv.at[1, 3 - d])

    @pl.loop(0, 4)
    def _(t):
        block = t + div(t, 2) - 2 * div(t, 3)

        @pl.when(t == 1)
        def _():
            norms_end(1)
            norms_start(2)
            take_query(1)
            take_query(3)

        @pl.when(t == 3)
        def _():
            stage_1()
            take_query(2)

        attend(block, 1, column, 1)

    @pl.loop(0, 11)
    def _(t):
        for when, stage in ((2, stage_2), (2, stage_3), (6, stage_4), (7, stage_5)):

            @pl.when(t == when)
            def _():
                stage()

        @pl.when(t == 0)
        def _():
            norms_end(2)
            norms_start(3)

        @pl.when(t == 5)
        def _():
            norms_end(3)

        u, v = div(t, 4), rem(t, 4)
        a, b = div(v, 2), 1 + 2 * rem(v, 2)
        is_0, is_1, is_2 = div((1 - u) * (2 - u), 2), u * (2 - u), div(u * (u - 1), 2)
        dx = is_0 * a * b + is_1 * (1 + 2 * a) + is_2 * (v + a)
        dz = is_0 * (1 - a) * b + is_1 * b + is_2 * 2
        at = column_at(dx, dz)
        arrived(part_of_sibling(kv, at, other), pair_recv.at[dx * 4 + dz])
        attend(0, 4, at, 1)

    for dz in range(4):
        arrived(part_of_sibling(kv, column_at(2, dz), other), pair_recv.at[8 + dz])

    def back(d):
        lanes = pl.ds(pl.multiple_of(y * ROWS, ROWS), ROWS)
        return (
            finished.at[d],
            out_ref.at[:, lanes],
            back_send.at[d - 1],
            back_recv.at[d - 1],
            line[d - 1],
        )

    @pl.loop(0, 4)
    def _(t):
        block = 2 - t + 3 * div(t, 2) - 2 * div(t, 3)
        attend(block, 1, rem(x + 2, 4) * 4, 4)
        row_sum = jnp.sum(sums[block], axis=1, keepdims=True)
        attended = (total[block] / row_sum).astype(BF16)
        for g in range(G):
            finished[block, :, g * D : (g + 1) * D] = attended[g * HALF : (g + 1) * HALF]
        for i, d in enumerate((2, 1, 3)):

            @pl.when(t == i)
            def _():
                send(lambda d=d: back(d))

    lanes = pl.ds(pl.multiple_of(y * ROWS, ROWS), ROWS)
    own = pltpu.make_async_copy(finished.at[0], out_ref.at[:, lanes], local_sem.at[0])
    own.start()
    for make in sent:
        pltpu.make_async_remote_copy(*make(), device_id_type=MESH).wait_send()
    own.wait()
    for d in (2, 1, 3):
        lanes = pl.ds(pl.multiple_of(rem(y + 4 - d, 4) * ROWS, ROWS), ROWS)
        arrived(out_ref.at[:, lanes], back_recv.at[d - 1])


def part_of_sibling(kv, at, other):
    return kv.at[at, other]


def attention(tokens, order, q, k, v):
    return pl.pallas_call(
        attention_kernel,
        out_shape=(
            jax.ShapeDtypeStruct((HALF, 4 * ROWS), BF16),
            jax.ShapeDtypeStruct((1,), jnp.int32),
        ),
        in_specs=[
            pl.BlockSpec(memory_space=pltpu.SMEM),
            pl.BlockSpec(memory_space=pltpu.SMEM),
            pl.BlockSpec(memory_space=pltpu.VMEM),
            pl.BlockSpec(memory_space=pltpu.VMEM),
            pl.BlockSpec(memory_space=pltpu.VMEM),
        ],
        out_specs=(
            pl.BlockSpec(memory_space=pltpu.VMEM),
            pl.BlockSpec(memory_space=pltpu.SMEM),
        ),
        scratch_shapes=[
            pltpu.VMEM((4 * G, HALF, D), BF16),
            pltpu.VMEM((4, 2, HALF, D), BF16),
            pltpu.VMEM((16, 2, 2, 4 * HALF, D), BF16),
            pltpu.VMEM((16, 2, 4 * HALF, D), BF16),
            pltpu.VMEM((4, G, HALF, D), BF16),
            pltpu.VMEM((4, HALF, D), BF16),
            pltpu.VMEM((4, ROWS, D), F32),
            pltpu.VMEM((4, ROWS, D), F32),
            pltpu.VMEM((4, HALF, ROWS), BF16),
            pltpu.SemaphoreType.DMA((2,)),
            pltpu.SemaphoreType.DMA((2, 3)),
            pltpu.SemaphoreType.DMA((2, 3)),
            pltpu.SemaphoreType.DMA((16, 7)),
            pltpu.SemaphoreType.DMA((16,)),
            pltpu.SemaphoreType.DMA((16,)),
            pltpu.SemaphoreType.DMA((16,)),
            pltpu.SemaphoreType.DMA((3,)),
            pltpu.SemaphoreType.DMA((3,)),
            pltpu.VMEM((4, 4, 8, D), F32),
            pltpu.SemaphoreType.DMA((4, 3)),
            pltpu.SemaphoreType.DMA((4, 3)),
        ],
        compiler_params=pltpu.CompilerParams(
            collective_id=0, has_side_effects=True, vmem_limit_bytes=VMEM_LIMIT
        ),
        name="attention",
    )(tokens, order, q, k, v)


negative = -1e30


def stretch_lookup(positions, stretch_ends):
    return jnp.sum((stretch_ends[None, :] <= positions[:, None]).astype(jnp.int32), axis=1)


def row_stretches(first_row, piece_rows, block_order, stretch_ends, block_rows):
    row_ids = first_row + jnp.arange(piece_rows, dtype=jnp.int32)
    slot_index = row_ids // block_rows
    slot_ids = jnp.arange(block_order.shape[0], dtype=jnp.int32)
    owners = jnp.sum(
        jnp.where(slot_index[:, None] == slot_ids[None, :], block_order[None, :], 0), axis=1
    )
    return stretch_lookup(owners * block_rows + row_ids % block_rows, stretch_ends)


def attend_tile(
    partial_value, query_part, query_stretch, key_part, value_part, key_stretch, score_scale
):
    run_max, run_sum, numerator = partial_value
    scores = (
        jnp.einsum("qhgd,khd->hgqk", query_part, key_part, preferred_element_type=jnp.float32)
        * score_scale
    )
    visible = key_stretch[None, :] <= query_stretch[:, None]
    masked = jnp.where(visible, scores, negative)
    new_max = jnp.maximum(run_max, jnp.max(masked, axis=-1))
    weights = jnp.where(visible, jnp.exp(masked - new_max[..., None]), 0.0)
    factor = jnp.exp(run_max - new_max)
    new_sum = run_sum * factor + jnp.sum(weights, axis=-1)
    product = jnp.einsum(
        "hgqk,khd->qhgd",
        weights.astype(jnp.bfloat16),
        value_part,
        preferred_element_type=jnp.float32,
    )
    new_numerator = numerator * jnp.transpose(factor, (2, 0, 1))[..., None] + product
    return (new_max, new_sum, new_numerator)


def empty_partial(length, kv_local, group_size, head_dim):
    return (
        jnp.full((kv_local, group_size, length), negative, jnp.float32),
        jnp.zeros((kv_local, group_size, length), jnp.float32),
        jnp.zeros((length, kv_local, group_size, head_dim), jnp.float32),
    )


def everywhere(x):
    copies = jnp.broadcast_to(x[None], (lax.axis_size("ctx"), *x.shape))
    return lax.all_to_all(copies, "ctx", split_axis=0, concat_axis=0).reshape(-1, *x.shape[1:])


def shifted_body(queries, keys, values, stretch_tokens, block_order):
    tok_rows, heads_query, head_dim = queries.shape
    heads_kv = keys.shape[1]
    group_size = heads_query // heads_kv
    uly_size = lax.axis_size("uly")
    row_count = tok_rows * uly_size
    block_rows = row_count // 2
    kv_local = heads_kv // uly_size
    score_scale = head_dim ** (-0.5)
    stretch_ends = jnp.cumsum(stretch_tokens)
    ctx_index = lax.axis_index("ctx")
    query_stretch = row_stretches(
        ctx_index * row_count, row_count, block_order, stretch_ends, block_rows
    )
    query_local, key_local, value_local = (
        lax.all_to_all(queries, "uly", split_axis=1, concat_axis=0, tiled=True),
        lax.all_to_all(keys, "uly", split_axis=1, concat_axis=0, tiled=True),
        lax.all_to_all(values, "uly", split_axis=1, concat_axis=0, tiled=True),
    )
    query_local = query_local.reshape(row_count, kv_local, group_size, head_dim)
    query_spans = ((0, row_count),)
    initial = tuple(
        (empty_partial(length, kv_local, group_size, head_dim) for offset, length in query_spans)
    )
    key_piece = everywhere(key_local)
    piece_rows = key_piece.shape[0]
    key_stretches = row_stretches(jnp.int32(0), piece_rows, block_order, stretch_ends, block_rows)
    tile_rows = math.gcd(piece_rows, 1024)
    tile_count = piece_rows // tile_rows
    stacked = (
        key_piece.reshape(tile_count, tile_rows, kv_local, head_dim),
        everywhere(value_local).reshape(
            tile_count, tile_rows, kv_local, head_dim
        ),
        key_stretches.reshape(tile_count, tile_rows),
    )

    def one_tile(partials, tile_parts):
        key_part, value_part, key_stretch = tile_parts
        updated = []
        for (offset, length), partial_value in zip(query_spans, partials):
            partial_value = attend_tile(
                partial_value,
                query_local,
                query_stretch,
                key_part,
                value_part,
                key_stretch,
                score_scale,
            )
            updated.append(partial_value)
        return (tuple(updated), None)

    result, unused = lax.scan(one_tile, initial, stacked)
    partials = result
    outputs = []
    for partial_value in partials:
        run_max, run_sum, numerator = partial_value
        outputs.append(numerator / jnp.transpose(run_sum, (2, 0, 1))[..., None])
    attended = outputs[0].astype(jnp.bfloat16)
    attended = attended.reshape(row_count, heads_query // uly_size, head_dim)
    returned = lax.all_to_all(attended, "uly", split_axis=0, concat_axis=1, tiled=True)
    return returned.reshape(tok_rows, heads_query * head_dim)


def body(queries, keys, values, stretch_tokens, block_order):
    attended, safe = attention(
        stretch_tokens, block_order, queries, keys, values
    )
    return lax.cond(
        safe[0] == 1,
        lambda: attended,
        lambda: shifted_body(queries, keys, values, stretch_tokens, block_order),
    )


def solution(mesh):
    return jax.shard_map(
        body,
        mesh=mesh,
        in_specs=(
            P(("ctx", "uly"), None, None),
            P(("ctx", "uly"), None, None),
            P(("ctx", "uly"), None, None),
            P(),
            P(),
        ),
        out_specs=P(("ctx", "uly"), None),
        check_vma=False,
    )
```

```python
import math

import jax
import jax.numpy as jnp
from jax import lax
from jax.experimental import pallas as pl
from jax.experimental.pallas import tpu as pltpu
from jax.sharding import PartitionSpec as P

MESH = pl.DeviceIdType.MESH
F32 = jnp.float32
BF16 = jnp.bfloat16

D = 128
G = 6
HALF = 128
SLOTS = 64
SLOT = 256
COLUMN = 1024
ROWS = G * HALF
TOKENS = SLOTS * SLOT
TO_LOG2 = (D**-0.5) * 1.4426950408889634
HIDDEN = -30000.0
SAFE_LOG2 = 90.0
VMEM_LIMIT = 60 * 2**20


def div(a, n):
    return lax.div(a, n)


def rem(a, n):
    return lax.rem(a, n)


def place():
    ctx, uly = lax.axis_index("ctx"), lax.axis_index("uly")
    return div(ctx, 8), div(uly, 2) * 2 + rem(ctx, 2), rem(div(ctx, 2), 4), rem(uly, 2)


def device_at(x, y, z, core):
    return (x * 8 + z * 2 + rem(y, 2), div(y, 2) * 2 + core)


def slot_in_column(chip):
    return 2 * rem(chip, 2) + div(chip, 2)


def stretch_ends(tokens_ref):
    first = tokens_ref[0]
    second = first + tokens_ref[1]
    return first, second, second + tokens_ref[2]


def stretch_of(position, ends):
    total = (position >= ends[0]).astype(jnp.int32)
    for end in ends[1:]:
        total = total + (position >= end).astype(jnp.int32)
    return total


def key_columns(first_position, rows, ends):
    position = first_position + lax.broadcasted_iota(jnp.int32, (rows, D), 0)
    lane = lax.broadcasted_iota(jnp.int32, (rows, D), 1)
    return jnp.where(lane < stretch_of(position, ends), HIDDEN, 0.0).astype(BF16)


def query_columns(first_position, rows, ends):
    position = first_position + lax.broadcasted_iota(jnp.int32, (rows, D), 0)
    lane = lax.broadcasted_iota(jnp.int32, (rows, D), 1)
    return jnp.where(lane == stretch_of(position, ends), 1.0, 0.0).astype(BF16)


def lane_sum(x):
    total = x[:, :D]
    for j in range(1, x.shape[1] // D):
        total = total + x[:, j * D : (j + 1) * D]
    return total


def largest_square(x):
    x = x.reshape(-1, D).astype(F32)
    return jnp.max(jnp.sum(x * x, axis=1, keepdims=True))


def scores_of(q, k):
    return lax.dot_general(q, k, (((1,), (1,)), ((), ())), preferred_element_type=F32)


def attention_kernel(
    tokens_ref,
    order_ref,
    q_in,
    k_in,
    v_in,
    out_ref,
    safe_ref,
    q_ref,
    kv_ref,
    kv,
    columns,
    query,
    marks,
    total,
    sums,
    finished,
    local_sem,
    line_send,
    line_recv,
    ring_send,
    ring_recv,
    pair_send,
    pair_recv,
    back_send,
    back_recv,
    norms,
    norm_send,
    norm_recv,
):
    x, y, z, core = place()
    other = 1 - core
    column = 4 * x + z
    ends = stretch_ends(tokens_ref)

    def column_at(dx, dz):
        return rem(x + dx, 4) * 4 + rem(z + dz, 4)

    a_step = [4 * (rem(x + d, 4) - x) * (1 - core) + (rem(z + d, 4) - z) * core for d in range(4)]
    b_step = [4 * (rem(x + d, 4) - x) * core + (rem(z + d, 4) - z) * (1 - core) for d in range(4)]

    def along(da, db):
        return da * (1 - core) + db * core, da * core + db * (1 - core)

    def chunk(da, db):
        return column + a_step[da] + b_step[db]

    y_low, here_uly = rem(y, 2), div(y, 2) * 2 + core

    def device_along(da, db):
        return (2 * chunk(da, db) + y_low, here_uly)

    line = [device_at(x, rem(y + d, 4), z, core) for d in (1, 2, 3)]
    ring = [device_along(*o) for o in ((1, 0), (3, 0), (0, 1), (0, 3))]
    sibling = device_at(x, y, z, other)

    barrier = pltpu.get_barrier_semaphore()
    across = [device_at(rem(x + 2, 4), y, z, core), device_at(x, y, rem(z + 2, 4), core)]
    for partner in (*line, *ring, sibling, *across):
        pl.semaphore_signal(barrier, inc=1, device_id=partner, device_id_type=MESH)
    kv_ref[:, 0] = jnp.swapaxes(k_in[...], 0, 1)
    kv_ref[:, 1] = jnp.swapaxes(v_in[...], 0, 1)
    q_ref[...] = jnp.swapaxes(q_in[...], 0, 1)
    upper = lax.broadcasted_iota(jnp.int32, (8, D), 0) < 4
    norms[0, 0] = jnp.where(upper, largest_square(q_in[...]), largest_square(k_in[...]))
    pl.semaphore_wait(barrier, 10)

    sent = []

    def send(make):
        pltpu.make_async_remote_copy(*make(), device_id_type=MESH).start()
        sent.append(make)

    stages = (
        [device_at(rem(x + d, 4), y, z, core) for d in (1, 2, 3)],
        [device_at(x, y, rem(z + d, 4), core) for d in (1, 2, 3)],
        [sibling],
        line,
    )

    def norms_start(stage):
        for i, device in enumerate(stages[stage]):
            send(
                lambda i=i, device=device: (
                    norms.at[stage, 0],
                    norms.at[stage, 1 + i],
                    norm_send.at[stage, i],
                    norm_recv.at[stage, i],
                    device,
                )
            )

    def norms_end(stage):
        largest = norms[stage, 0]
        for i in range(len(stages[stage])):
            arrived(norms.at[stage, 1 + i], norm_recv.at[stage, i])
            largest = jnp.maximum(largest, norms[stage, 1 + i])
        if stage < 3:
            norms[stage + 1, 0] = largest
        else:
            safe = (largest[0, 0] * largest[4, 0] < (SAFE_LOG2 / TO_LOG2) ** 2).astype(jnp.int32)
            safe_ref[0] = safe

    norms_start(0)

    def slab(chip):
        rows = pl.ds(pl.multiple_of(slot_in_column(chip) * HALF, HALF), HALF)
        return kv.at[column, core, :, rows]

    ys = [y] + [rem(y + d, 4) for d in (1, 2, 3)]
    for d in (1, 3, 2):
        send(
            lambda d=d: (
                kv_ref.at[ys[d]],
                slab(y),
                line_send.at[0, d - 1],
                line_recv.at[0, d - 1],
                line[d - 1],
            )
        )
    own_kv = pltpu.make_async_copy(kv_ref.at[y], slab(y), local_sem.at[0])
    own_kv.start()
    def send_query(d):
        send(
            lambda: (
                q_ref.at[pl.ds(G * ys[d], G)],
                query.at[4 - d],
                line_send.at[1, d - 1],
                line_recv.at[1, d - 1],
                line[d - 1],
            )
        )

    own_q = pltpu.make_async_copy(q_ref.at[pl.ds(G * y, G)], query.at[0], local_sem.at[1])
    own_q.start()

    def arrived(dst, sem):
        pltpu.make_async_copy(dst, dst, sem).wait()

    def part(da, db):
        return kv.at[chunk(da, db), core]

    def hop(da, db, step_a, step_b):
        there = (da - step_a) % 4 * 4 + (db - step_b) % 4

        def make():
            src = part(da, db)
            return (
                src,
                src,
                ring_send.at[da * 4 + db, step_a if step_a else 3 + step_b],
                ring_recv.at[there],
                device_along(step_a, step_b),
            )

        send(make)

    def near_a():
        hop(0, 0, 1, 0)
        hop(0, 0, 3, 0)

    def near_b(da):
        hop(da, 0, 0, 1)
        hop(da, 0, 0, 3)

    def far_b(da):
        hop(da, 0, 0, 2)

    def take(da, db):
        arrived(part(da, db), ring_recv.at[da * 4 + db])

    def share(da, db):
        def make():
            dx, dz = along(da, db)
            src = part(da, db)
            at = dx * 4 + dz
            return src, src, pair_send.at[at], pair_recv.at[at], sibling

        send(make)

    def take_and_share(*offsets):
        for offset in offsets:
            take(*offset)
            share(*offset)

    def stage_0():
        near_a()
        near_b(0)
        share(0, 0)

    def stage_1():
        take(1, 0)
        take(3, 0)
        hop(0, 0, 2, 0)
        near_b(1)
        near_b(3)
        share(1, 0)
        share(3, 0)
        take_and_share((0, 1), (0, 3))

    def stage_2():
        take_and_share((1, 1), (1, 3), (3, 1), (3, 3))
        for da in (0, 1, 3):
            far_b(da)

    def stage_3():
        take(2, 0)
        near_b(2)
        far_b(2)
        share(2, 0)

    def stage_4():
        take_and_share((0, 2), (1, 2), (3, 2))

    def stage_5():
        take_and_share((2, 1), (2, 3), (2, 2))

    @pl.loop(0, 16)
    def _(at):
        for j in range(4):
            extra = key_columns(order_ref[at * 4 + j] * SLOT, SLOT, ends)
            for half in range(2):
                rows = slice(j * HALF, (j + 1) * HALF)
                columns[at, half, rows] = extra[half * HALF : (half + 1) * HALF]

    send_query(1)
    send_query(3)

    for d in (1, 3, 2):
        arrived(slab(ys[4 - d]), line_recv.at[0, d - 1])
    own_kv.wait()
    norms_end(0)
    norms_start(1)
    send_query(2)
    stage_0()

    for d in range(4):
        slot = column * 4 + slot_in_column(rem(y + d, 4))
        marks[d] = query_columns(order_ref[slot] * SLOT + core * HALF, HALF, ends)
    total[...] = jnp.zeros_like(total)
    sums[...] = jnp.zeros_like(sums)

    def attend(block, blocks, at, count):
        there = pl.ds(at, count)
        k = kv[there, :, 0].reshape(count * COLUMN, D)
        v = kv[there, :, 1].reshape(count * COLUMN, D)
        extra = columns[there].reshape(count * COLUMN, D)
        k = jnp.concatenate([k, extra], axis=1)
        here = pl.ds(block, blocks)
        q = query[here].reshape(blocks * ROWS, D)
        mark = jnp.broadcast_to(marks[here][:, None], (blocks, G, HALF, D))
        q = jnp.concatenate([q, mark.reshape(blocks * ROWS, D)], axis=1)
        weights = jnp.exp2(scores_of(q, k) * TO_LOG2)
        sums[here] += lane_sum(weights).reshape(blocks, ROWS, D)
        product = jnp.dot(weights.astype(BF16), v, preferred_element_type=F32)
        total[here] += product.reshape(blocks, ROWS, D)

    own_q.wait()
    arrived(part_of_sibling(kv, column, other), pair_recv.at[0])

    def take_query(d):
        arrived(query.at[d], line_recv.at[1, 3 - d])

    @pl.loop(0, 4)
    def _(t):
        block = t + div(t, 2) - 2 * div(t, 3)

        @pl.when(t == 1)
        def _():
            norms_end(1)
            norms_start(2)
            take_query(1)
            take_query(3)

        @pl.when(t == 3)
        def _():
            stage_1()
            take_query(2)

        attend(block, 1, column, 1)

    @pl.loop(0, 8)
    def _(t):
        for when, stage in ((2, stage_2), (2, stage_3), (6, stage_4), (7, stage_5)):

            @pl.when(t == when)
            def _():
                stage()

        @pl.when(t == 0)
        def _():
            norms_end(2)
            norms_start(3)

        @pl.when(t == 5)
        def _():
            norms_end(3)

        u, v = div(t, 4), rem(t, 4)
        a, b = div(v, 2), 1 + 2 * rem(v, 2)
        dx = (1 - u) * a * b + u * (1 + 2 * a)
        dz = (1 - u) * (1 - a) * b + u * b
        at = column_at(dx, dz)
        arrived(part_of_sibling(kv, at, other), pair_recv.at[dx * 4 + dz])
        attend(0, 4, at, 1)

    def last_column(t):
        dx = t + div(t, 2)
        at = column_at(dx, 2)
        return dx, at

    @pl.loop(0, 3)
    def _(t):
        dx, at = last_column(t)
        arrived(part_of_sibling(kv, at, other), pair_recv.at[dx * 4 + 2])
        attend(1, 3, at, 1)

    for dz in range(4):
        arrived(part_of_sibling(kv, column_at(2, dz), other), pair_recv.at[8 + dz])

    def finish(block):
        row_sum = jnp.sum(sums[block], axis=1, keepdims=True)
        attended = (total[block] / row_sum).astype(BF16)
        for g in range(G):
            finished[block, :, g * D : (g + 1) * D] = attended[g * HALF : (g + 1) * HALF]

    def back(d):
        lanes = pl.ds(pl.multiple_of(y * ROWS, ROWS), ROWS)
        return (
            finished.at[d],
            out_ref.at[:, lanes],
            back_send.at[d - 1],
            back_recv.at[d - 1],
            line[d - 1],
        )

    @pl.loop(0, 4)
    def _(t):
        block = 2 - t + 3 * div(t, 2) - 2 * div(t, 3)
        attend(block, 1, rem(x + 2, 4) * 4, 4)
        for i, d in enumerate((2, 1, 3)):

            @pl.when(t == i)
            def _():
                finish(d)
                send(lambda d=d: back(d))

    @pl.loop(0, 3)
    def _(t):
        attend(0, 1, last_column(t)[1], 1)

    finish(0)
    lanes = pl.ds(pl.multiple_of(y * ROWS, ROWS), ROWS)
    own = pltpu.make_async_copy(finished.at[0], out_ref.at[:, lanes], local_sem.at[0])
    own.start()
    for make in sent:
        pltpu.make_async_remote_copy(*make(), device_id_type=MESH).wait_send()
    own.wait()
    for d in (2, 1, 3):
        lanes = pl.ds(pl.multiple_of(rem(y + 4 - d, 4) * ROWS, ROWS), ROWS)
        arrived(out_ref.at[:, lanes], back_recv.at[d - 1])


def part_of_sibling(kv, at, other):
    return kv.at[at, other]


def attention(tokens, order, q, k, v):
    return pl.pallas_call(
        attention_kernel,
        out_shape=(
            jax.ShapeDtypeStruct((HALF, 4 * ROWS), BF16),
            jax.ShapeDtypeStruct((1,), jnp.int32),
        ),
        in_specs=[
            pl.BlockSpec(memory_space=pltpu.SMEM),
            pl.BlockSpec(memory_space=pltpu.SMEM),
            pl.BlockSpec(memory_space=pltpu.VMEM),
            pl.BlockSpec(memory_space=pltpu.VMEM),
            pl.BlockSpec(memory_space=pltpu.VMEM),
        ],
        out_specs=(
            pl.BlockSpec(memory_space=pltpu.VMEM),
            pl.BlockSpec(memory_space=pltpu.SMEM),
        ),
        scratch_shapes=[
            pltpu.VMEM((4 * G, HALF, D), BF16),
            pltpu.VMEM((4, 2, HALF, D), BF16),
            pltpu.VMEM((16, 2, 2, 4 * HALF, D), BF16),
            pltpu.VMEM((16, 2, 4 * HALF, D), BF16),
            pltpu.VMEM((4, G, HALF, D), BF16),
            pltpu.VMEM((4, HALF, D), BF16),
            pltpu.VMEM((4, ROWS, D), F32),
            pltpu.VMEM((4, ROWS, D), F32),
            pltpu.VMEM((4, HALF, ROWS), BF16),
            pltpu.SemaphoreType.DMA((2,)),
            pltpu.SemaphoreType.DMA((2, 3)),
            pltpu.SemaphoreType.DMA((2, 3)),
            pltpu.SemaphoreType.DMA((16, 7)),
            pltpu.SemaphoreType.DMA((16,)),
            pltpu.SemaphoreType.DMA((16,)),
            pltpu.SemaphoreType.DMA((16,)),
            pltpu.SemaphoreType.DMA((3,)),
            pltpu.SemaphoreType.DMA((3,)),
            pltpu.VMEM((4, 4, 8, D), F32),
            pltpu.SemaphoreType.DMA((4, 3)),
            pltpu.SemaphoreType.DMA((4, 3)),
        ],
        compiler_params=pltpu.CompilerParams(
            collective_id=0, has_side_effects=True, vmem_limit_bytes=VMEM_LIMIT
        ),
        name="attention",
    )(tokens, order, q, k, v)


negative = -1e30


def stretch_lookup(positions, stretch_ends):
    return jnp.sum((stretch_ends[None, :] <= positions[:, None]).astype(jnp.int32), axis=1)


def row_stretches(first_row, piece_rows, block_order, stretch_ends, block_rows):
    row_ids = first_row + jnp.arange(piece_rows, dtype=jnp.int32)
    slot_index = row_ids // block_rows
    slot_ids = jnp.arange(block_order.shape[0], dtype=jnp.int32)
    owners = jnp.sum(
        jnp.where(slot_index[:, None] == slot_ids[None, :], block_order[None, :], 0), axis=1
    )
    return stretch_lookup(owners * block_rows + row_ids % block_rows, stretch_ends)


def attend_tile(
    partial_value, query_part, query_stretch, key_part, value_part, key_stretch, score_scale
):
    run_max, run_sum, numerator = partial_value
    scores = (
        jnp.einsum("qhgd,khd->hgqk", query_part, key_part, preferred_element_type=jnp.float32)
        * score_scale
    )
    visible = key_stretch[None, :] <= query_stretch[:, None]
    masked = jnp.where(visible, scores, negative)
    new_max = jnp.maximum(run_max, jnp.max(masked, axis=-1))
    weights = jnp.where(visible, jnp.exp(masked - new_max[..., None]), 0.0)
    factor = jnp.exp(run_max - new_max)
    new_sum = run_sum * factor + jnp.sum(weights, axis=-1)
    product = jnp.einsum(
        "hgqk,khd->qhgd",
        weights.astype(jnp.bfloat16),
        value_part,
        preferred_element_type=jnp.float32,
    )
    new_numerator = numerator * jnp.transpose(factor, (2, 0, 1))[..., None] + product
    return (new_max, new_sum, new_numerator)


def empty_partial(length, kv_local, group_size, head_dim):
    return (
        jnp.full((kv_local, group_size, length), negative, jnp.float32),
        jnp.zeros((kv_local, group_size, length), jnp.float32),
        jnp.zeros((length, kv_local, group_size, head_dim), jnp.float32),
    )


def everywhere(x):
    copies = jnp.broadcast_to(x[None], (lax.axis_size("ctx"), *x.shape))
    return lax.all_to_all(copies, "ctx", split_axis=0, concat_axis=0).reshape(-1, *x.shape[1:])


def shifted_body(queries, keys, values, stretch_tokens, block_order):
    tok_rows, heads_query, head_dim = queries.shape
    heads_kv = keys.shape[1]
    group_size = heads_query // heads_kv
    uly_size = lax.axis_size("uly")
    row_count = tok_rows * uly_size
    block_rows = row_count // 2
    kv_local = heads_kv // uly_size
    score_scale = head_dim ** (-0.5)
    stretch_ends = jnp.cumsum(stretch_tokens)
    ctx_index = lax.axis_index("ctx")
    query_stretch = row_stretches(
        ctx_index * row_count, row_count, block_order, stretch_ends, block_rows
    )
    query_local, key_local, value_local = (
        lax.all_to_all(queries, "uly", split_axis=1, concat_axis=0, tiled=True),
        lax.all_to_all(keys, "uly", split_axis=1, concat_axis=0, tiled=True),
        lax.all_to_all(values, "uly", split_axis=1, concat_axis=0, tiled=True),
    )
    query_local = query_local.reshape(row_count, kv_local, group_size, head_dim)
    query_spans = ((0, row_count),)
    initial = tuple(
        (empty_partial(length, kv_local, group_size, head_dim) for offset, length in query_spans)
    )
    key_piece = everywhere(key_local)
    piece_rows = key_piece.shape[0]
    key_stretches = row_stretches(jnp.int32(0), piece_rows, block_order, stretch_ends, block_rows)
    tile_rows = math.gcd(piece_rows, 1024)
    tile_count = piece_rows // tile_rows
    stacked = (
        key_piece.reshape(tile_count, tile_rows, kv_local, head_dim),
        everywhere(value_local).reshape(
            tile_count, tile_rows, kv_local, head_dim
        ),
        key_stretches.reshape(tile_count, tile_rows),
    )

    def one_tile(partials, tile_parts):
        key_part, value_part, key_stretch = tile_parts
        updated = []
        for (offset, length), partial_value in zip(query_spans, partials):
            partial_value = attend_tile(
                partial_value,
                query_local,
                query_stretch,
                key_part,
                value_part,
                key_stretch,
                score_scale,
            )
            updated.append(partial_value)
        return (tuple(updated), None)

    result, unused = lax.scan(one_tile, initial, stacked)
    partials = result
    outputs = []
    for partial_value in partials:
        run_max, run_sum, numerator = partial_value
        outputs.append(numerator / jnp.transpose(run_sum, (2, 0, 1))[..., None])
    attended = outputs[0].astype(jnp.bfloat16)
    attended = attended.reshape(row_count, heads_query // uly_size, head_dim)
    returned = lax.all_to_all(attended, "uly", split_axis=0, concat_axis=1, tiled=True)
    return returned.reshape(tok_rows, heads_query * head_dim)


def body(queries, keys, values, stretch_tokens, block_order):
    attended, safe = attention(
        stretch_tokens, block_order, queries, keys, values
    )
    return lax.cond(
        safe[0] == 1,
        lambda: attended,
        lambda: shifted_body(queries, keys, values, stretch_tokens, block_order),
    )


def solution(mesh):
    return jax.shard_map(
        body,
        mesh=mesh,
        in_specs=(
            P(("ctx", "uly"), None, None),
            P(("ctx", "uly"), None, None),
            P(("ctx", "uly"), None, None),
            P(),
            P(),
        ),
        out_specs=P(("ctx", "uly"), None),
        check_vma=False,
    )
```

```python
import math

import jax
import jax.numpy as jnp
from jax import lax
from jax.experimental import pallas as pl
from jax.experimental.pallas import tpu as pltpu
from jax.sharding import PartitionSpec as P

MESH = pl.DeviceIdType.MESH
F32 = jnp.float32
BF16 = jnp.bfloat16

D = 128
G = 6
HALF = 128
SLOTS = 64
SLOT = 256
COLUMN = 1024
ROWS = G * HALF
TOKENS = SLOTS * SLOT
TO_LOG2 = (D**-0.5) * 1.4426950408889634
HIDDEN = -30000.0
SAFE_LOG2 = 90.0
VMEM_LIMIT = 60 * 2**20


def div(a, n):
    return lax.div(a, n)


def rem(a, n):
    return lax.rem(a, n)


def place():
    ctx, uly = lax.axis_index("ctx"), lax.axis_index("uly")
    return div(ctx, 8), div(uly, 2) * 2 + rem(ctx, 2), rem(div(ctx, 2), 4), rem(uly, 2)


def device_at(x, y, z, core):
    return (x * 8 + z * 2 + rem(y, 2), div(y, 2) * 2 + core)


def slot_in_column(chip):
    return 2 * rem(chip, 2) + div(chip, 2)


def stretch_ends(tokens_ref):
    first = tokens_ref[0]
    second = first + tokens_ref[1]
    return first, second, second + tokens_ref[2]


def stretch_of(position, ends):
    total = (position >= ends[0]).astype(jnp.int32)
    for end in ends[1:]:
        total = total + (position >= end).astype(jnp.int32)
    return total


def key_columns(first_position, rows, ends):
    position = first_position + lax.broadcasted_iota(jnp.int32, (rows, D), 0)
    lane = lax.broadcasted_iota(jnp.int32, (rows, D), 1)
    return jnp.where(lane < stretch_of(position, ends), HIDDEN, 0.0).astype(BF16)


def query_columns(first_position, rows, ends):
    position = first_position + lax.broadcasted_iota(jnp.int32, (rows, D), 0)
    lane = lax.broadcasted_iota(jnp.int32, (rows, D), 1)
    return jnp.where(lane == stretch_of(position, ends), 1.0, 0.0).astype(BF16)


def lane_sum(x):
    total = x[:, :D]
    for j in range(1, x.shape[1] // D):
        total = total + x[:, j * D : (j + 1) * D]
    return total


def largest_square(x):
    x = x.reshape(-1, D).astype(F32)
    return jnp.max(jnp.sum(x * x, axis=1, keepdims=True))


def scores_of(q, k):
    return lax.dot_general(q, k, (((1,), (1,)), ((), ())), preferred_element_type=F32)


def attention_kernel(
    tokens_ref,
    order_ref,
    q_in,
    k_in,
    v_in,
    out_ref,
    safe_ref,
    q_ref,
    kv_ref,
    kv,
    columns,
    query,
    marks,
    total,
    sums,
    finished,
    local_sem,
    line_send,
    line_recv,
    ring_send,
    ring_recv,
    pair_send,
    pair_recv,
    back_send,
    back_recv,
    norms,
    norm_send,
    norm_recv,
):
    x, y, z, core = place()
    other = 1 - core
    column = 4 * x + z
    ends = stretch_ends(tokens_ref)

    def column_at(dx, dz):
        return rem(x + dx, 4) * 4 + rem(z + dz, 4)

    a_step = [4 * (rem(x + d, 4) - x) * (1 - core) + (rem(z + d, 4) - z) * core for d in range(4)]
    b_step = [4 * (rem(x + d, 4) - x) * core + (rem(z + d, 4) - z) * (1 - core) for d in range(4)]

    def along(da, db):
        return da * (1 - core) + db * core, da * core + db * (1 - core)

    def chunk(da, db):
        return column + a_step[da] + b_step[db]

    y_low, here_uly = rem(y, 2), div(y, 2) * 2 + core

    def device_along(da, db):
        return (2 * chunk(da, db) + y_low, here_uly)

    line = [device_at(x, rem(y + d, 4), z, core) for d in (1, 2, 3)]
    ring = [device_along(*o) for o in ((1, 0), (3, 0), (0, 1), (0, 3))]
    sibling = device_at(x, y, z, other)

    barrier = pltpu.get_barrier_semaphore()
    across = [device_at(rem(x + 2, 4), y, z, core), device_at(x, y, rem(z + 2, 4), core)]
    for partner in (*line, *ring, sibling, *across):
        pl.semaphore_signal(barrier, inc=1, device_id=partner, device_id_type=MESH)
    kv_ref[:, 0] = jnp.swapaxes(k_in[...], 0, 1)
    kv_ref[:, 1] = jnp.swapaxes(v_in[...], 0, 1)
    q_ref[...] = jnp.swapaxes(q_in[...], 0, 1)
    upper = lax.broadcasted_iota(jnp.int32, (8, D), 0) < 4
    norms[0, 0] = jnp.where(upper, largest_square(q_in[...]), largest_square(k_in[...]))
    pl.semaphore_wait(barrier, 10)

    sent = []

    def send(make):
        pltpu.make_async_remote_copy(*make(), device_id_type=MESH).start()
        sent.append(make)

    stages = (
        [device_at(rem(x + d, 4), y, z, core) for d in (1, 2, 3)],
        [device_at(x, y, rem(z + d, 4), core) for d in (1, 2, 3)],
        [sibling],
        line,
    )

    def norms_start(stage):
        for i, device in enumerate(stages[stage]):
            send(
                lambda i=i, device=device: (
                    norms.at[stage, 0],
                    norms.at[stage, 1 + i],
                    norm_send.at[stage, i],
                    norm_recv.at[stage, i],
                    device,
                )
            )

    def norms_end(stage):
        largest = norms[stage, 0]
        for i in range(len(stages[stage])):
            arrived(norms.at[stage, 1 + i], norm_recv.at[stage, i])
            largest = jnp.maximum(largest, norms[stage, 1 + i])
        if stage < 3:
            norms[stage + 1, 0] = largest
        else:
            safe = (largest[0, 0] * largest[4, 0] < (SAFE_LOG2 / TO_LOG2) ** 2).astype(jnp.int32)
            safe_ref[0] = safe

    norms_start(0)

    def slab(chip):
        rows = pl.ds(pl.multiple_of(slot_in_column(chip) * HALF, HALF), HALF)
        return kv.at[column, core, :, rows]

    ys = [y] + [rem(y + d, 4) for d in (1, 2, 3)]
    for d in (1, 3, 2):
        send(
            lambda d=d: (
                kv_ref.at[ys[d]],
                slab(y),
                line_send.at[0, d - 1],
                line_recv.at[0, d - 1],
                line[d - 1],
            )
        )
    own_kv = pltpu.make_async_copy(kv_ref.at[y], slab(y), local_sem.at[0])
    own_kv.start()
    def send_query(d):
        send(
            lambda: (
                q_ref.at[pl.ds(G * ys[d], G)],
                query.at[4 - d],
                line_send.at[1, d - 1],
                line_recv.at[1, d - 1],
                line[d - 1],
            )
        )

    own_q = pltpu.make_async_copy(q_ref.at[pl.ds(G * y, G)], query.at[0], local_sem.at[1])
    own_q.start()

    def arrived(dst, sem):
        pltpu.make_async_copy(dst, dst, sem).wait()

    def part(da, db):
        return kv.at[chunk(da, db), core]

    def hop(da, db, step_a, step_b):
        there = (da - step_a) % 4 * 4 + (db - step_b) % 4

        def make():
            src = part(da, db)
            return (
                src,
                src,
                ring_send.at[da * 4 + db, step_a if step_a else 3 + step_b],
                ring_recv.at[there],
                device_along(step_a, step_b),
            )

        send(make)

    def near_a():
        hop(0, 0, 1, 0)
        hop(0, 0, 3, 0)

    def near_b(da):
        hop(da, 0, 0, 1)
        hop(da, 0, 0, 3)

    def far_b(da):
        hop(da, 0, 0, 2)

    def take(da, db):
        arrived(part(da, db), ring_recv.at[da * 4 + db])

    def share(da, db):
        def make():
            dx, dz = along(da, db)
            src = part(da, db)
            at = dx * 4 + dz
            return src, src, pair_send.at[at], pair_recv.at[at], sibling

        send(make)

    def take_and_share(*offsets):
        for offset in offsets:
            take(*offset)
            share(*offset)

    def stage_0():
        near_a()
        near_b(0)
        share(0, 0)

    def stage_1():
        take(1, 0)
        take(3, 0)
        hop(0, 0, 2, 0)
        near_b(1)
        near_b(3)
        share(1, 0)
        share(3, 0)
        take_and_share((0, 1), (0, 3))

    def stage_2():
        take_and_share((1, 1), (1, 3), (3, 1), (3, 3))
        for da in (0, 1, 3):
            far_b(da)

    def stage_3():
        take(2, 0)
        near_b(2)
        far_b(2)
        share(2, 0)

    def stage_4():
        take_and_share((0, 2), (1, 2), (3, 2))

    def stage_5():
        take_and_share((2, 1), (2, 3), (2, 2))

    @pl.loop(0, 16)
    def _(at):
        for j in range(4):
            extra = key_columns(order_ref[at * 4 + j] * SLOT, SLOT, ends)
            for half in range(2):
                rows = slice(j * HALF, (j + 1) * HALF)
                columns[at, half, rows] = extra[half * HALF : (half + 1) * HALF]

    send_query(1)
    send_query(3)

    for d in (1, 3, 2):
        arrived(slab(ys[4 - d]), line_recv.at[0, d - 1])
    own_kv.wait()
    norms_end(0)
    norms_start(1)
    send_query(2)
    stage_0()

    for d in range(4):
        slot = column * 4 + slot_in_column(rem(y + d, 4))
        marks[d] = query_columns(order_ref[slot] * SLOT + core * HALF, HALF, ends)
    total[...] = jnp.zeros_like(total)
    sums[...] = jnp.zeros_like(sums)

    def attend(block, blocks, at, count):
        there = pl.ds(at, count)
        k = kv[there, :, 0].reshape(count * COLUMN, D)
        v = kv[there, :, 1].reshape(count * COLUMN, D)
        extra = columns[there].reshape(count * COLUMN, D)
        k = jnp.concatenate([k, extra], axis=1)
        here = pl.ds(block, blocks)
        q = query[here].reshape(blocks * ROWS, D)
        mark = jnp.broadcast_to(marks[here][:, None], (blocks, G, HALF, D))
        q = jnp.concatenate([q, mark.reshape(blocks * ROWS, D)], axis=1)
        weights = jnp.exp2(scores_of(q, k) * TO_LOG2)
        sums[here] += lane_sum(weights).reshape(blocks, ROWS, D)
        product = jnp.dot(weights.astype(BF16), v, preferred_element_type=F32)
        total[here] += product.reshape(blocks, ROWS, D)

    own_q.wait()
    arrived(part_of_sibling(kv, column, other), pair_recv.at[0])

    def take_query(d):
        arrived(query.at[d], line_recv.at[1, 3 - d])

    @pl.loop(0, 4)
    def _(t):
        block = t + div(t, 2) - 2 * div(t, 3)

        @pl.when(t == 1)
        def _():
            norms_end(1)
            norms_start(2)
            take_query(1)
            take_query(3)

        @pl.when(t == 3)
        def _():
            stage_1()
            take_query(2)

        attend(block, 1, column, 1)

    @pl.loop(0, 8)
    def _(t):
        for when, stage in ((2, stage_2), (2, stage_3), (6, stage_4), (7, stage_5)):

            @pl.when(t == when)
            def _():
                stage()

        @pl.when(t == 0)
        def _():
            norms_end(2)
            norms_start(3)

        @pl.when(t == 5)
        def _():
            norms_end(3)

        u, v = div(t, 4), rem(t, 4)
        a, b = div(v, 2), 1 + 2 * rem(v, 2)
        dx = (1 - u) * a * b + u * (1 + 2 * a)
        dz = (1 - u) * (1 - a) * b + u * b
        at = column_at(dx, dz)
        arrived(part_of_sibling(kv, at, other), pair_recv.at[dx * 4 + dz])
        attend(0, 4, at, 1)

    def last_column(t):
        dx = t + div(t, 2)
        at = column_at(dx, 2)
        return dx, at

    @pl.loop(0, 3)
    def _(t):
        dx, at = last_column(t)
        arrived(part_of_sibling(kv, at, other), pair_recv.at[dx * 4 + 2])
        attend(1, 3, at, 1)

    for dz in range(4):
        arrived(part_of_sibling(kv, column_at(2, dz), other), pair_recv.at[8 + dz])

    def finish(block):
        row_sum = jnp.sum(sums[block], axis=1, keepdims=True)
        attended = (total[block] / row_sum).astype(BF16)
        for g in range(G):
            finished[block, :, g * D : (g + 1) * D] = attended[g * HALF : (g + 1) * HALF]

    def back(d):
        lanes = pl.ds(pl.multiple_of(y * ROWS, ROWS), ROWS)
        return (
            finished.at[d],
            out_ref.at[:, lanes],
            back_send.at[d - 1],
            back_recv.at[d - 1],
            line[d - 1],
        )

    @pl.loop(0, 4)
    def _(t):
        block = 2 - t + 3 * div(t, 2) - 2 * div(t, 3)
        attend(block, 1, rem(x + 2, 4) * 4, 4)
        for i, d in enumerate((2, 1, 3)):

            @pl.when(t == i)
            def _():
                finish(d)
                send(lambda d=d: back(d))

    @pl.loop(0, 3)
    def _(t):
        attend(0, 1, last_column(t)[1], 1)

    row_sum = jnp.sum(sums[0], axis=1, keepdims=True)
    attended = (total[0] / row_sum).astype(BF16)
    for g in range(G):
        lanes = pl.ds(pl.multiple_of(y * ROWS + g * D, D), D)
        out_ref[:, lanes] = attended[g * HALF : (g + 1) * HALF]
    for make in sent:
        pltpu.make_async_remote_copy(*make(), device_id_type=MESH).wait_send()
    for d in (2, 1, 3):
        lanes = pl.ds(pl.multiple_of(rem(y + 4 - d, 4) * ROWS, ROWS), ROWS)
        arrived(out_ref.at[:, lanes], back_recv.at[d - 1])


def part_of_sibling(kv, at, other):
    return kv.at[at, other]


def attention(tokens, order, q, k, v):
    return pl.pallas_call(
        attention_kernel,
        out_shape=(
            jax.ShapeDtypeStruct((HALF, 4 * ROWS), BF16),
            jax.ShapeDtypeStruct((1,), jnp.int32),
        ),
        in_specs=[
            pl.BlockSpec(memory_space=pltpu.SMEM),
            pl.BlockSpec(memory_space=pltpu.SMEM),
            pl.BlockSpec(memory_space=pltpu.VMEM),
            pl.BlockSpec(memory_space=pltpu.VMEM),
            pl.BlockSpec(memory_space=pltpu.VMEM),
        ],
        out_specs=(
            pl.BlockSpec(memory_space=pltpu.VMEM),
            pl.BlockSpec(memory_space=pltpu.SMEM),
        ),
        scratch_shapes=[
            pltpu.VMEM((4 * G, HALF, D), BF16),
            pltpu.VMEM((4, 2, HALF, D), BF16),
            pltpu.VMEM((16, 2, 2, 4 * HALF, D), BF16),
            pltpu.VMEM((16, 2, 4 * HALF, D), BF16),
            pltpu.VMEM((4, G, HALF, D), BF16),
            pltpu.VMEM((4, HALF, D), BF16),
            pltpu.VMEM((4, ROWS, D), F32),
            pltpu.VMEM((4, ROWS, D), F32),
            pltpu.VMEM((4, HALF, ROWS), BF16),
            pltpu.SemaphoreType.DMA((2,)),
            pltpu.SemaphoreType.DMA((2, 3)),
            pltpu.SemaphoreType.DMA((2, 3)),
            pltpu.SemaphoreType.DMA((16, 7)),
            pltpu.SemaphoreType.DMA((16,)),
            pltpu.SemaphoreType.DMA((16,)),
            pltpu.SemaphoreType.DMA((16,)),
            pltpu.SemaphoreType.DMA((3,)),
            pltpu.SemaphoreType.DMA((3,)),
            pltpu.VMEM((4, 4, 8, D), F32),
            pltpu.SemaphoreType.DMA((4, 3)),
            pltpu.SemaphoreType.DMA((4, 3)),
        ],
        compiler_params=pltpu.CompilerParams(
            collective_id=0, has_side_effects=True, vmem_limit_bytes=VMEM_LIMIT
        ),
        name="attention",
    )(tokens, order, q, k, v)


negative = -1e30


def stretch_lookup(positions, stretch_ends):
    return jnp.sum((stretch_ends[None, :] <= positions[:, None]).astype(jnp.int32), axis=1)


def row_stretches(first_row, piece_rows, block_order, stretch_ends, block_rows):
    row_ids = first_row + jnp.arange(piece_rows, dtype=jnp.int32)
    slot_index = row_ids // block_rows
    slot_ids = jnp.arange(block_order.shape[0], dtype=jnp.int32)
    owners = jnp.sum(
        jnp.where(slot_index[:, None] == slot_ids[None, :], block_order[None, :], 0), axis=1
    )
    return stretch_lookup(owners * block_rows + row_ids % block_rows, stretch_ends)


def attend_tile(
    partial_value, query_part, query_stretch, key_part, value_part, key_stretch, score_scale
):
    run_max, run_sum, numerator = partial_value
    scores = (
        jnp.einsum("qhgd,khd->hgqk", query_part, key_part, preferred_element_type=jnp.float32)
        * score_scale
    )
    visible = key_stretch[None, :] <= query_stretch[:, None]
    masked = jnp.where(visible, scores, negative)
    new_max = jnp.maximum(run_max, jnp.max(masked, axis=-1))
    weights = jnp.where(visible, jnp.exp(masked - new_max[..., None]), 0.0)
    factor = jnp.exp(run_max - new_max)
    new_sum = run_sum * factor + jnp.sum(weights, axis=-1)
    product = jnp.einsum(
        "hgqk,khd->qhgd",
        weights.astype(jnp.bfloat16),
        value_part,
        preferred_element_type=jnp.float32,
    )
    new_numerator = numerator * jnp.transpose(factor, (2, 0, 1))[..., None] + product
    return (new_max, new_sum, new_numerator)


def empty_partial(length, kv_local, group_size, head_dim):
    return (
        jnp.full((kv_local, group_size, length), negative, jnp.float32),
        jnp.zeros((kv_local, group_size, length), jnp.float32),
        jnp.zeros((length, kv_local, group_size, head_dim), jnp.float32),
    )


def everywhere(x):
    copies = jnp.broadcast_to(x[None], (lax.axis_size("ctx"), *x.shape))
    return lax.all_to_all(copies, "ctx", split_axis=0, concat_axis=0).reshape(-1, *x.shape[1:])


def shifted_body(queries, keys, values, stretch_tokens, block_order):
    tok_rows, heads_query, head_dim = queries.shape
    heads_kv = keys.shape[1]
    group_size = heads_query // heads_kv
    uly_size = lax.axis_size("uly")
    row_count = tok_rows * uly_size
    block_rows = row_count // 2
    kv_local = heads_kv // uly_size
    score_scale = head_dim ** (-0.5)
    stretch_ends = jnp.cumsum(stretch_tokens)
    ctx_index = lax.axis_index("ctx")
    query_stretch = row_stretches(
        ctx_index * row_count, row_count, block_order, stretch_ends, block_rows
    )
    query_local, key_local, value_local = (
        lax.all_to_all(queries, "uly", split_axis=1, concat_axis=0, tiled=True),
        lax.all_to_all(keys, "uly", split_axis=1, concat_axis=0, tiled=True),
        lax.all_to_all(values, "uly", split_axis=1, concat_axis=0, tiled=True),
    )
    query_local = query_local.reshape(row_count, kv_local, group_size, head_dim)
    query_spans = ((0, row_count),)
    initial = tuple(
        (empty_partial(length, kv_local, group_size, head_dim) for offset, length in query_spans)
    )
    key_piece = everywhere(key_local)
    piece_rows = key_piece.shape[0]
    key_stretches = row_stretches(jnp.int32(0), piece_rows, block_order, stretch_ends, block_rows)
    tile_rows = math.gcd(piece_rows, 1024)
    tile_count = piece_rows // tile_rows
    stacked = (
        key_piece.reshape(tile_count, tile_rows, kv_local, head_dim),
        everywhere(value_local).reshape(
            tile_count, tile_rows, kv_local, head_dim
        ),
        key_stretches.reshape(tile_count, tile_rows),
    )

    def one_tile(partials, tile_parts):
        key_part, value_part, key_stretch = tile_parts
        updated = []
        for (offset, length), partial_value in zip(query_spans, partials):
            partial_value = attend_tile(
                partial_value,
                query_local,
                query_stretch,
                key_part,
                value_part,
                key_stretch,
                score_scale,
            )
            updated.append(partial_value)
        return (tuple(updated), None)

    result, unused = lax.scan(one_tile, initial, stacked)
    partials = result
    outputs = []
    for partial_value in partials:
        run_max, run_sum, numerator = partial_value
        outputs.append(numerator / jnp.transpose(run_sum, (2, 0, 1))[..., None])
    attended = outputs[0].astype(jnp.bfloat16)
    attended = attended.reshape(row_count, heads_query // uly_size, head_dim)
    returned = lax.all_to_all(attended, "uly", split_axis=0, concat_axis=1, tiled=True)
    return returned.reshape(tok_rows, heads_query * head_dim)


def body(queries, keys, values, stretch_tokens, block_order):
    attended, safe = attention(
        stretch_tokens, block_order, queries, keys, values
    )
    return lax.cond(
        safe[0] == 1,
        lambda: attended,
        lambda: shifted_body(queries, keys, values, stretch_tokens, block_order),
    )


def solution(mesh):
    return jax.shard_map(
        body,
        mesh=mesh,
        in_specs=(
            P(("ctx", "uly"), None, None),
            P(("ctx", "uly"), None, None),
            P(("ctx", "uly"), None, None),
            P(),
            P(),
        ),
        out_specs=P(("ctx", "uly"), None),
        check_vma=False,
    )
```
